256 devices in a mesh: ctx: 64 (over z, y, core), head: 4 (over x).
Axes of the slice: x: 4, y: 4, z: 8, core: 2. Of those that a mesh axis runs over, the one named last changes fastest.
Arguments:
- queries: bfloat16 [24576, 64, 128], P('ctx', 'head'), may hold values from -12 to 12
- keys: bfloat16 [8, 262144, 128], P('head', 'ctx'), may hold values from -8 to 8
- values: bfloat16 [8, 262144, 128], P('head', 'ctx'), may hold values from -6 to 6
- sel_blocks: int32 [384, 8, 16], P('ctx', 'head'), may hold values from 0 to 4095, as said below
- sel_counts: int32 [384, 8], P('ctx', 'head'), may hold values from 8 to 16, as said below
Outputs:
- attended: bfloat16 [24576, 8192], P(('ctx', 'head'))
The draws below stay inside these ranges and needn't reach their ends.
Inputs may be any that keep to these rules, and one draw needn't show every extreme that they name: For each (b, g) the first sel_counts[b, g] entries of sel_blocks[b, g] are distinct; later entries are arbitrary block numbers that are not used. The rows of one device are the (b, g) with equal b // 6 and equal g // 2: of the used entries of one device's rows, at most 6 name blocks j with equal j // 64, and on every device some value of j // 64 gets exactly 6. `sel_counts`: among the rows of each device at least one (b, g) has the count 16.
All inputs are finite; a program needn't handle non-finite values.
Results may differ from the reference program's by a relative error of at most 0.0049.
Values may be sent and summed in bfloat16 or wider, within the bound.
A program may use at most 128 MiB of HBM per device.

```python
import jax
import jax.numpy as jnp
from jax import lax

HEADS = 64
GROUPS = 8
HD = 128
BLK = 64
SEL = 16
QB_DEV = 6
HPG = 8
G_DEV = 2
KB_DEV = 64
CAP = 6
QB = 384
QT = 24576
KEYS = 262144
KB = 4096
N_CTX = 64
N_HEAD = 4


def draw_queries(key, part):
    streams = jax.random.split(jax.random.fold_in(key, 7), 1)
    entries = 2.0 * jnp.clip(jax.random.normal(streams[0], (QT, HEADS, HD), jnp.float32), -4.0, 4.0)
    return entries.astype(jnp.bfloat16)


def draw_keys(key, part):
    streams = jax.random.split(jax.random.fold_in(key, 9), 1)
    entries = jnp.clip(jax.random.normal(streams[0], (GROUPS, KEYS, HD), jnp.float32), -4.0, 4.0)
    return entries.astype(jnp.bfloat16)


def selection_lists(key):
    seeded = jax.random.fold_in(key, 23)
    item_count = QB_DEV * G_DEV
    slot_count = item_count * SEL

    def one_device(device):
        streams = jax.random.split(jax.random.fold_in(seeded, device), 7)
        counts = jax.random.randint(streams[0], (item_count,), SEL // 2, SEL + 1)
        filled = jax.random.randint(streams[1], (), 0, item_count)
        counts = jnp.where(jnp.arange(item_count) == filled, SEL, counts).astype(jnp.int32)
        slot_ids = jnp.arange(slot_count)
        live_slot = slot_ids % SEL < jnp.repeat(counts, SEL)
        priority = jax.random.permutation(streams[2], slot_count).astype(jnp.int32)
        ranking = priority + jnp.where(live_slot, 0, slot_count).astype(jnp.int32)
        ordering = jnp.argsort(ranking, stable=True)
        standing = jnp.argsort(ordering, stable=True).astype(jnp.int32)
        bucket = jnp.minimum(standing // CAP, N_CTX - 1)
        holders = jax.random.permutation(streams[3], N_CTX).astype(jnp.int32)
        holder = holders[bucket]
        offsets = jax.random.randint(streams[4], (N_CTX,), 0, KB_DEV)
        shuffle = jax.random.permutation(streams[5], KB_DEV).astype(jnp.int32)
        inside = shuffle[(offsets[bucket] + standing % CAP) % KB_DEV]
        picked = holder * KB_DEV + inside
        filler = jax.random.randint(streams[6], (slot_count,), 0, KB)
        blocks = jnp.where(live_slot, picked, filler).astype(jnp.int32)
        return (blocks.reshape(QB_DEV, G_DEV, SEL), counts.reshape(QB_DEV, G_DEV))
    devices = jnp.arange(N_CTX * N_HEAD)
    blocks, counts = jax.vmap(one_device)(devices)
    blocks = blocks.reshape(N_CTX, N_HEAD, QB_DEV, G_DEV, SEL).transpose(0, 2, 1, 3, 4).reshape(QB_DEV * N_CTX, GROUPS, SEL)
    counts = counts.reshape(N_CTX, N_HEAD, QB_DEV, G_DEV).transpose(0, 2, 1, 3).reshape(QB_DEV * N_CTX, GROUPS)
    return (blocks, counts)


def draw_sel_blocks(key, part):
    return selection_lists(key)[0]


def draw_sel_counts(key, part):
    return selection_lists(key)[1]


def steps_of(own_key, extent, cuts, least, top_value):
    factor_of, own = 1.0, jax.random.fold_in(own_key, 6)
    for position, parts in cuts:
        heights = jnp.exp(jax.random.uniform(jax.random.fold_in(own, position), (parts,), jnp.float32, least / len(cuts), top_value / len(cuts)))
        factor_of = factor_of * jnp.repeat(heights, extent[position] // parts).reshape([-1 if axis == position else 1 for axis in range(len(extent))])
    return factor_of


def centred(key, extent, width, reach, cuts=(), held_as=jnp.bfloat16):
    values = width * jax.random.normal(key, extent, jnp.float32)
    if cuts:
        values = values * steps_of(key, extent, cuts, -0.22, 0.18)
    return jnp.clip(values, -reach, reach).astype(held_as)


def setup_inputs(seed: int = 0) -> dict:
    key_of = jax.random.split(jax.random.key(seed), 6)
    return {
        "queries": draw_queries(jax.random.fold_in(key_of[5], 71), 0),
        "keys": draw_keys(jax.random.fold_in(key_of[5], 71), 0),
        "values": centred(key_of[2], (GROUPS, KEYS, HD), 1.0, 6.0, ((0, 4), (1, 64))),
        "sel_blocks": draw_sel_blocks(jax.random.fold_in(key_of[5], 71), 0),
        "sel_counts": draw_sel_counts(jax.random.fold_in(key_of[5], 71), 0),
    }


def weighting(query_rows, key_rows, kept_keys, scaling):
    scores = jnp.dot(query_rows, key_rows.T, preferred_element_type=jnp.float32) * scaling
    scores = jnp.where(kept_keys[None, :], scores, -jnp.inf)
    largest = jnp.max(scores, axis=1, keepdims=True)
    exponent = jnp.exp(scores - largest)
    return (exponent / jnp.sum(exponent, axis=1, keepdims=True)).astype(jnp.bfloat16)


def attend(query_rows, key_rows, value_rows, kept_keys, scaling):
    weights = weighting(query_rows, key_rows, kept_keys, scaling)
    return jnp.dot(weights, value_rows, preferred_element_type=jnp.float32).astype(jnp.bfloat16)


def reference(queries, keys, values, sel_blocks, sel_counts):
    scaling = HD ** -0.5
    key_tiles = keys.reshape(GROUPS, KB, BLK, HD)
    value_tiles = values.reshape(GROUPS, KB, BLK, HD)
    query_blocks = queries.reshape(QB, BLK, GROUPS, HPG, HD)
    group_ids = jnp.arange(GROUPS)

    def one_block(index):
        query_rows = query_blocks[index].transpose(1, 0, 2, 3).reshape(GROUPS, BLK * HPG, HD)
        chosen = sel_blocks[index]
        counts = sel_counts[index]
        key_sel = key_tiles[group_ids[:, None], chosen].reshape(GROUPS, SEL * BLK, HD)
        value_sel = value_tiles[group_ids[:, None], chosen].reshape(GROUPS, SEL * BLK, HD)
        kept_keys = (jnp.arange(SEL * BLK)[None, :] // BLK) < counts[:, None]
        output = jax.vmap(attend, in_axes=(0, 0, 0, 0, None))(query_rows, key_sel, value_sel, kept_keys, scaling)
        return output.reshape(GROUPS, BLK, HPG, HD).transpose(1, 0, 2, 3).reshape(BLK, HEADS * HD)

    result = lax.map(one_block, jnp.arange(QB))
    return result.reshape(QT, HEADS * HD)
```

```python
import jax
import jax.numpy as jnp
import numpy as np
from jax import lax
from jax.experimental import pallas as pl
from jax.experimental.pallas import tpu as pltpu
from jax.sharding import PartitionSpec as P

BLK = 64
HD = 128
SEL = 16
ITEMS = 12
NZ = 8
NW = 8
STEPS = 4
USUAL = (108, 84, 56, 24)
FULL = (168, 120, 72, 24)
MESH = pl.DeviceIdType.MESH


def at_ctx(index):
    return {"ctx": index}


def requests_kernel(mine, k_own, table, k_twin, local_sem, send_sem, recv_sem):
    me = lax.axis_index("ctx")
    z, w = me // NW, me % NW
    barrier = pltpu.get_barrier_semaphore()
    for r in range(1, 8):
        pl.semaphore_signal(barrier, inc=1, device_id=at_ctx(z * NW + (w + r) % NW), device_id_type=MESH)
        pl.semaphore_signal(barrier, inc=1, device_id=at_ctx((z + r) % NZ * NW + w), device_id_type=MESH)
    pl.semaphore_wait(barrier, 14)

    own = pltpu.make_async_copy(mine.at[pl.ds(w, 1)], table.at[pl.ds(w, 1)], local_sem)
    own.start()
    inside = []
    for r in range(1, NW):
        ow = (w + r) % NW
        copy = pltpu.make_async_remote_copy(
            src_ref=mine.at[pl.ds(ow, 1)], dst_ref=table.at[pl.ds(w, 1)],
            send_sem=send_sem.at[r], recv_sem=recv_sem.at[r],
            device_id=at_ctx(z * NW + ow), device_id_type=MESH,
        )
        copy.start()
        inside.append(copy)
    twin = me + 1 - 2 * (me % 2)
    keys_over = pltpu.make_async_remote_copy(
        src_ref=k_own, dst_ref=k_twin, send_sem=send_sem.at[0], recv_sem=recv_sem.at[0],
        device_id=at_ctx(twin), device_id_type=MESH,
    )
    keys_over.start()
    own.wait()
    for copy in inside:
        copy.wait()
    along = []
    for r in range(1, NZ):
        copy = pltpu.make_async_remote_copy(
            src_ref=table.at[pl.ds(0, NW)], dst_ref=table.at[pl.ds((NZ - r) * NW, NW)],
            send_sem=send_sem.at[NW + r], recv_sem=recv_sem.at[NW + r],
            device_id=at_ctx((z + r) % NZ * NW + w), device_id_type=MESH,
        )
        copy.start()
        along.append(copy)
    for copy in along:
        copy.wait()
    keys_over.wait()


def exchange_requests(mine, k_own):
    vmem, anywhere = pl.BlockSpec(memory_space=pltpu.VMEM), pl.BlockSpec(memory_space=pl.ANY)
    return pl.pallas_call(
        requests_kernel,
        out_shape=(
            jax.ShapeDtypeStruct((NZ * NW, 1, 128), jnp.int32),
            jax.ShapeDtypeStruct(k_own.shape, k_own.dtype),
        ),
        in_specs=[vmem, anywhere],
        out_specs=(vmem, anywhere),
        scratch_shapes=[
            pltpu.SemaphoreType.DMA,
            pltpu.SemaphoreType.DMA((16,)),
            pltpu.SemaphoreType.DMA((16,)),
        ],
        compiler_params=pltpu.CompilerParams(collective_id=0, has_side_effects=True),
        name="requests",
    )(mine, k_own)


def tiles_kernel(caps, arrays, fetch, src, post, over, *refs):
    cuts = (0, *caps[::-1])
    refs = list(refs)
    take = lambda n: [refs.pop(0) for _ in range(n)]
    owns = take(arrays)
    twins = [None if f else refs.pop(0) for f in fetch]
    outs, over_out = take(arrays), refs.pop(0)
    tab, lists, stage = take(arrays), take(arrays), take(arrays)
    hops = [take(STEPS) for _ in range(arrays)]
    overs, tab_sem, twin_send, z_send, z_recv, y_send, y_recv, y_local, over_send, over_recv = refs
    me = lax.axis_index("ctx")
    z, w = me // NW, me % NW
    core = me % 2
    twin_at = me + 1 - 2 * core
    towards = (((z + 1) % NZ) * NW + w, ((z + NZ - 1) % NZ) * NW + w)

    barrier = pltpu.get_barrier_semaphore()
    for other in towards:
        pl.semaphore_signal(barrier, inc=1, device_id=at_ctx(other), device_id_type=MESH)
    for r in range(1, NW):
        pl.semaphore_signal(barrier, inc=1, device_id=at_ctx(z * NW + (w + r) % NW), device_id_type=MESH)
    pl.semaphore_wait(barrier, NW + 1)

    loads = []
    for a in range(arrays):
        mine = tab[a].at[pl.ds(core * 128, 128)]
        pair = [pltpu.make_async_copy(owns[a], mine, tab_sem.at[a, 0])]
        if fetch[a]:
            pair.append(
                pltpu.make_async_remote_copy(
                    src_ref=owns[a], dst_ref=mine, send_sem=twin_send.at[a], recv_sem=tab_sem.at[a, 1],
                    device_id=at_ctx(twin_at), device_id_type=MESH,
                )
            )
        else:
            pair.append(
                pltpu.make_async_copy(twins[a], tab[a].at[pl.ds((1 - core) * 128, 128)], tab_sem.at[a, 1])
            )
        for copy in pair:
            copy.start()
        loads.append(pair)
    told = []
    for r in range(1, NW):
        copy = pltpu.make_async_remote_copy(
            src_ref=over, dst_ref=overs.at[r], send_sem=over_send.at[r], recv_sem=over_recv.at[r],
            device_id=at_ctx(z * NW + (w + r) % NW), device_id_type=MESH,
        )
        copy.start()
        told.append(copy)

    def hop(a, d, step, piece):
        lo, hi = cuts[piece], cuts[piece + 1]
        source = lists[a] if step == 1 else hops[a][step - 2]
        number = (0, 4, 7, 9)[step - 1] + piece
        return pltpu.make_async_remote_copy(
            src_ref=source.at[d, pl.ds(lo, hi - lo)],
            dst_ref=hops[a][step - 1].at[d, pl.ds(lo, hi - lo)],
            send_sem=z_send.at[a, d, number],
            recv_sem=z_recv.at[a, d, number],
            device_id=at_ctx(towards[d]),
            device_id_type=MESH,
        )

    def pack(a, piece):
        for d in range(2):
            def one(i, carry):
                lists[a][d, i] = tab[a][src[d * caps[0] + i]]
                return carry

            lax.fori_loop(cuts[piece], cuts[piece + 1], one, 0)

    def deliver(a, k):
        base = k * NW * 6
        if k == 4:
            def both(i, carry):
                at = base + i
                for d in range(2):
                    for s in range(6):
                        stage[a][base + (2 * i + d) * 6 + s] = hops[a][3][d, post[base + (2 * i + d) * 6 + s]]
                return carry

            lax.fori_loop(0, NW // 2, both, 0)
        else:
            def one(i, carry):
                index = post[base + i]
                if k == 0:
                    tile = tab[a][index]
                elif k < 4:
                    tile = hops[a][k - 1][0, index]
                else:
                    tile = hops[a][7 - k][1, index]
                stage[a][base + i] = tile
                return carry

            lax.fori_loop(0, NW * 6, one, 0)

        def send(r, carry):
            ow = (w + r) % NW
            pltpu.make_async_remote_copy(
                src_ref=stage[a].at[pl.ds(base + ow * 6, 6)],
                dst_ref=outs[a].at[pl.ds(base + w * 6, 6)],
                send_sem=y_send.at[a],
                recv_sem=y_recv.at[a],
                device_id=at_ctx(z * NW + ow),
                device_id_type=MESH,
            ).start()
            return carry

        lax.fori_loop(1, NW, send, 0)
        pltpu.make_async_copy(
            stage[a].at[pl.ds(base + w * 6, 6)], outs[a].at[pl.ds(base + w * 6, 6)], y_local.at[a]
        ).start()

    def arrive_and_pass(a, step):
        for piece in range(5 - step):
            for d in range(2):
                hop(a, d, step, piece).wait_recv()
                if piece < 4 - step:
                    hop(a, d, step + 1, piece).start()

    def start_first(a):
        for piece in range(STEPS):
            for d in range(2):
                hop(a, d, 1, piece).start()

    for copy in loads[0]:
        copy.wait()
    for piece in range(STEPS):
        pack(0, piece)
        for d in range(2):
            hop(0, d, 1, piece).start()
    if arrays == 2:
        for copy in loads[1]:
            copy.wait()
        for piece in range(STEPS):
            pack(1, piece)
    deliver(0, 0)
    arrive_and_pass(0, 1)
    if arrays == 2:
        start_first(1)
        deliver(1, 0)
    for a in range(arrays):
        if a:
            arrive_and_pass(a, 1)
        for step in range(1, STEPS):
            deliver(a, step)
            deliver(a, NZ - step)
            arrive_and_pass(a, step + 1)
        deliver(a, STEPS)
    for a in range(arrays):
        for d in range(2):
            for step in range(1, STEPS + 1):
                for piece in range(STEPS + 1 - step):
                    hop(a, d, step, piece).wait_send()
    most = over[...]
    for r, copy in enumerate(told):
        copy.wait()
        most = jnp.maximum(most, overs[r + 1])
    over_out[...] = most
    remote, local = NZ * (NW - 1) * 6, NZ * 6
    for a in range(arrays):
        pltpu.make_async_copy(stage[a].at[pl.ds(0, remote)], stage[a].at[pl.ds(0, remote)], y_send.at[a]).wait()
        pltpu.make_async_copy(outs[a].at[pl.ds(0, remote)], outs[a].at[pl.ds(0, remote)], y_recv.at[a]).wait()
        pltpu.make_async_copy(outs[a].at[pl.ds(0, local)], outs[a].at[pl.ds(0, local)], y_local.at[a]).wait()


def exchange_tiles(number, caps, src, post, over, owns, twins):
    n = len(owns)
    fetch = tuple(t is None for t in twins)
    given = [t for t in twins if t is not None]
    tiles = jax.ShapeDtypeStruct((NZ * NW * 6, BLK, HD), owns[0].dtype)
    vmem = lambda *shape: pltpu.VMEM((*shape, BLK, HD), jnp.bfloat16)
    smem, whole = pl.BlockSpec(memory_space=pltpu.SMEM), pl.BlockSpec(memory_space=pltpu.VMEM)
    anywhere = pl.BlockSpec(memory_space=pl.ANY)
    dma = pltpu.SemaphoreType.DMA
    return pl.pallas_call(
        lambda *refs: tiles_kernel(caps, n, fetch, *refs),
        out_shape=(*[tiles] * n, jax.ShapeDtypeStruct((1, 128), jnp.int32)),
        in_specs=[smem, smem, whole, *[anywhere] * (n + len(given))],
        out_specs=(*[anywhere] * n, whole),
        scratch_shapes=[
            *[vmem(256)] * n,
            *[vmem(2, caps[0])] * n,
            *[vmem(NZ * NW * 6)] * n,
            *[vmem(2, c) for c in caps] * n,
            pltpu.VMEM((NW, 1, 128), jnp.int32),
            dma((n, 2)), dma((n,)), dma((n, 2, 10)), dma((n, 2, 10)),
            dma((n,)), dma((n,)), dma((n,)), dma((NW,)), dma((NW,)),
        ],
        compiler_params=pltpu.CompilerParams(
            collective_id=number, has_side_effects=True, vmem_limit_bytes=60 * 2**20
        ),
        name="tiles",
    )(src, post, over, *owns, *given)


def attend_kernel(where, counts, over, q, k, v, out, over_out, merged, qf, kc, vc, overs, send_sem, recv_sem, own_sem, over_send, over_recv):
    me = lax.axis_index("head")
    barrier = pltpu.get_barrier_semaphore()
    for r in range(1, 4):
        pl.semaphore_signal(barrier, inc=1, device_id={"head": (me + r) % 4}, device_id_type=MESH)
    pl.semaphore_wait(barrier, 3)
    told = []
    for r in range(1, 4):
        copy = pltpu.make_async_remote_copy(
            src_ref=over, dst_ref=overs.at[r], send_sem=over_send.at[r], recv_sem=over_recv.at[r],
            device_id={"head": (me + r) % 4}, device_id_type=MESH,
        )
        copy.start()
        told.append(copy)
    keys = SEL * BLK
    factor = float(HD ** -0.5 * np.log2(np.e))
    vc[:, HD:] = jnp.ones((keys, HD), jnp.bfloat16)
    first = ((me + 1) * 3 // 2) % 6

    def one_block(i, carry):
        b = (first + i) % 6
        qf[...] = q[pl.ds(b * BLK, BLK)].astype(jnp.float32).reshape(BLK * 16, HD)
        for g in range(2):
            item = b * 2 + g

            def gather(s, c):
                at = where[item * SEL + s]
                kc[pl.ds(s * BLK, BLK)] = k[at]
                vc[pl.ds(s * BLK, BLK), 0:HD] = v[at]
                return c

            lax.fori_loop(0, SEL, gather, 0)
            rows = jnp.concatenate(
                [qf[pl.ds(g * 8 + h, BLK, stride=16)].astype(jnp.bfloat16) for h in range(8)], axis=0
            )
            s = lax.dot_general(rows, kc[...], (((1,), (1,)), ((), ())), preferred_element_type=jnp.float32)
            kept = lax.broadcasted_iota(jnp.int32, (1, keys), 1) < counts[item] * BLK
            s = jnp.where(kept, s, -jnp.inf)
            top = jnp.max(s, axis=1, keepdims=True)
            p = jnp.exp2((s - top) * factor).astype(jnp.bfloat16)
            o = jnp.dot(p, vc[...], preferred_element_type=jnp.float32)
            o = o[:, 0:HD] / o[:, HD:]
            for h in range(8):
                merged[pl.ds(b * BLK, BLK), pl.ds(g * 1024 + h * HD, HD)] = o[h * BLK:(h + 1) * BLK].astype(jnp.bfloat16)
        for half in range(2):
            unit = b * 2 + half
            to = unit // 3
            source = merged.at[pl.ds(unit * 32, 32)]
            target = out.at[pl.ds((unit % 3) * 32, 32), pl.ds(pl.multiple_of(me * 2048, 2048), 2048)]

            @pl.when(to == me)
            def _():
                pltpu.make_async_copy(source, target, own_sem).start()

            @pl.when(to != me)
            def _():
                pltpu.make_async_remote_copy(
                    src_ref=source, dst_ref=target, send_sem=send_sem, recv_sem=recv_sem,
                    device_id={"head": to}, device_id_type=MESH,
                ).start()
        return carry

    lax.fori_loop(0, 6, one_block, 0)
    most = over[...]
    for r, copy in enumerate(told):
        copy.wait()
        most = jnp.maximum(most, overs[r + 1])
    over_out[...] = most
    pltpu.make_async_copy(out.at[:, pl.ds(0, 2048)], out.at[:, pl.ds(0, 2048)], own_sem).wait()
    pltpu.make_async_copy(out.at[:, pl.ds(0, 6144)], out.at[:, pl.ds(0, 6144)], send_sem).wait()
    pltpu.make_async_copy(out.at[:, pl.ds(0, 6144)], out.at[:, pl.ds(0, 6144)], recv_sem).wait()


def attend_all(number, where, counts, over, queries, k, v):
    smem, vmem = pl.BlockSpec(memory_space=pltpu.SMEM), pl.BlockSpec(memory_space=pltpu.VMEM)
    dma = pltpu.SemaphoreType.DMA
    return pl.pallas_call(
        attend_kernel,
        out_shape=(jax.ShapeDtypeStruct((96, 8192), jnp.bfloat16), jax.ShapeDtypeStruct((1, 128), jnp.int32)),
        in_specs=[smem, smem, vmem, vmem, vmem, vmem],
        out_specs=(pl.BlockSpec(memory_space=pl.ANY), vmem),
        scratch_shapes=[
            pltpu.VMEM((384, 2048), jnp.bfloat16),
            pltpu.VMEM((BLK * 16, HD), jnp.float32),
            pltpu.VMEM((SEL * BLK, HD), jnp.bfloat16),
            pltpu.VMEM((SEL * BLK, 2 * HD), jnp.bfloat16),
            pltpu.VMEM((4, 1, 128), jnp.int32),
            dma, dma, dma, dma((4,)), dma((4,)),
        ],
        compiler_params=pltpu.CompilerParams(
            collective_id=number, has_side_effects=True, vmem_limit_bytes=60 * 2**20
        ),
        name="attend",
    )(where, counts, over, queries, k, v)


def own_requests(blocks, counts):
    me = lax.axis_index("ctx")
    z = me // NW
    flat = blocks.reshape(-1)
    ids = np.arange(ITEMS * SEL)
    live = (jnp.asarray(ids % SEL)[None, :].reshape(ITEMS, SEL) < counts.reshape(ITEMS, 1)).reshape(-1)
    holder = jnp.where(live, flat // BLK, -1)
    earlier = jnp.asarray(ids[None, :] < ids[:, None])
    rank = jnp.sum(((holder[:, None] == holder[None, :]) & earlier).astype(jnp.int32), axis=1)
    core = holder % 2
    lane = (holder // 2 % 4) * 2 + (rank + core) % 2
    away = (z - holder // NW + NZ) % NZ
    inside = core * 3 + rank // 2
    tile = core * 128 + jnp.asarray(ids // SEL % 2) * BLK + flat % BLK + 1
    slot = jnp.where(live, lane * 48 + away * 6 + inside, -1)
    mine = jnp.sum(jnp.where(slot[None, :] == jnp.arange(NW * 48)[:, None], tile[None, :], 0), axis=1)
    mine = jnp.pad(mine.reshape(NW, 1, 48), ((0, 0), (0, 0), (0, 80)))
    where = jnp.where(live, away * 48 + lane * 6 + inside, 0)
    return mine, where


def plan(table, caps):
    asked = table.reshape(NZ, NW, 128)[:, :, :48].reshape(NZ, NW, NZ, 6)
    by_k = [jnp.roll(asked[:, :, k], -k, axis=0) for k in range(NZ)]
    up = [by_k[4][:, 0::2], by_k[3], by_k[2], by_k[1]]
    down = [by_k[4][:, 1::2], by_k[5], by_k[6], by_k[7]]
    lists = jnp.stack([jnp.concatenate([e.reshape(NZ, -1) for e in way], axis=1) for way in (up, down)])
    live = lists > 0
    size = lists.shape[2]
    before = jnp.asarray(np.triu(np.ones((size, size), np.float32), 1))
    at = jnp.dot(live.reshape(-1, size).astype(jnp.float32), before).astype(jnp.int32).reshape(lists.shape)
    hit = (at[:, 0, None, :] == jnp.arange(caps[0])[None, :, None]) & live[:, 0, None, :]
    src = jnp.maximum(jnp.sum(jnp.where(hit, lists[:, 0, None, :], 0), axis=2) - 1, 0)
    ends = np.cumsum([24, 48, 48, 48])
    totals = [jnp.sum(live[:, :, :e].astype(jnp.int32), axis=2) for e in ends]
    over = jnp.stack([jnp.max(t) > c for t, c in zip(totals, caps[::-1])]).any()

    def seg(d, k, part):
        lo, hi = (0, 24) if part == 0 else (24 + 48 * (part - 1), 24 + 48 * part)
        return jnp.minimum(at[d, (NZ - k) % NZ, lo:hi], caps[3 - part] - 1)

    here = jnp.maximum(by_k[0][0].reshape(-1) - 1, 0)
    four = jnp.stack([seg(0, 4, 0).reshape(4, 6), seg(1, 4, 0).reshape(4, 6)], axis=1).reshape(-1)
    post = jnp.concatenate(
        [here, seg(0, 1, 3), seg(0, 2, 2), seg(0, 3, 1), four, seg(1, 5, 1), seg(1, 6, 2), seg(1, 7, 3)]
    )
    return src.reshape(-1), post, over


def per_device(queries, keys, values, sel_blocks, sel_counts):
    k_own = keys.reshape(128, BLK, HD)
    v_own = values.reshape(128, BLK, HD)
    mine, where = own_requests(sel_blocks, sel_counts)
    counts = sel_counts.reshape(-1)
    table, k_twin = exchange_requests(mine, k_own)
    src, post, over = plan(table, USUAL)
    over = jnp.broadcast_to(over.astype(jnp.int32), (1, 128))
    k, v, over = exchange_tiles(1, USUAL, src, post, over, (k_own, v_own), (k_twin, None))
    out, over = attend_all(2, where, counts, over, queries, k, v)

    def again():
        src, post, _ = plan(table, FULL)
        none = jnp.zeros((1, 128), jnp.int32)
        k, _ = exchange_tiles(3, FULL, src, post, none, (k_own,), (None,))
        v, _ = exchange_tiles(4, FULL, src, post, none, (v_own,), (None,))
        return attend_all(5, where, counts, none, queries, k, v)[0]

    return lax.cond(over[0, 0] > 0, again, lambda: out)


def solution(mesh):
    placed = (
        P("ctx", "head", None),
        P("head", "ctx", None),
        P("head", "ctx", None),
        P("ctx", "head", None),
        P("ctx", "head"),
    )
    return jax.shard_map(
        per_device, mesh=mesh, in_specs=placed, out_specs=P(("ctx", "head"), None), check_vma=False
    )
```

```python
import jax
import jax.numpy as jnp
import numpy as np
from jax import lax
from jax.experimental import pallas as pl
from jax.experimental.pallas import tpu as pltpu
from jax.sharding import PartitionSpec as P

BLK = 64
HD = 128
SEL = 16
ITEMS = 12
NZ = 8
NW = 8
STEPS = 4
USUAL = (104, 78, 50, 24)
FULL = (168, 120, 72, 24)
MESH = pl.DeviceIdType.MESH


def at_ctx(index):
    return {"ctx": index}


def requests_kernel(
    mine, kinds, within, same, lower, column, k_own,
    table, src, post, over, k_twin,
    rows, local_sem, send_sem, recv_sem,
):
    me = lax.axis_index("ctx")
    z, w = me // NW, me % NW
    barrier = pltpu.get_barrier_semaphore()
    for r in range(1, 8):
        pl.semaphore_signal(barrier, inc=1, device_id=at_ctx(z * NW + (w + r) % NW), device_id_type=MESH)
        pl.semaphore_signal(barrier, inc=1, device_id=at_ctx((z + r) % NZ * NW + w), device_id_type=MESH)
    pl.semaphore_wait(barrier, 14)

    own = pltpu.make_async_copy(mine.at[pl.ds(w, 1)], rows.at[pl.ds(w, 1)], local_sem)
    own.start()
    inside = []
    for r in range(1, NW):
        ow = (w + r) % NW
        copy = pltpu.make_async_remote_copy(
            src_ref=mine.at[pl.ds(ow, 1)], dst_ref=rows.at[pl.ds(w, 1)],
            send_sem=send_sem.at[r], recv_sem=recv_sem.at[r],
            device_id=at_ctx(z * NW + ow), device_id_type=MESH,
        )
        copy.start()
        inside.append(copy)
    keys_over = pltpu.make_async_remote_copy(
        src_ref=k_own, dst_ref=k_twin, send_sem=send_sem.at[0], recv_sem=recv_sem.at[0],
        device_id=at_ctx(me + 1 - 2 * (me % 2)), device_id_type=MESH,
    )
    keys_over.start()
    own.wait()
    for copy in inside:
        copy.wait()
    table[0] = jnp.concatenate([rows[i] for i in range(NW)], axis=0)
    along = []
    for r in range(1, NZ):
        copy = pltpu.make_async_remote_copy(
            src_ref=table.at[0], dst_ref=table.at[NZ - r],
            send_sem=send_sem.at[NW + r], recv_sem=recv_sem.at[NW + r],
            device_id=at_ctx((z + r) % NZ * NW + w), device_id_type=MESH,
        )
        copy.start()
        along.append(copy)
    for copy in along:
        copy.wait()

    kind = kinds[...]
    asked = [table[i] for i in range(NZ)]
    by_source = []
    for i in range(NZ):
        row = jnp.zeros((NW, 128), jnp.int32)
        for k in range(NZ):
            row = jnp.where(kind == k, asked[(i + k) % NZ], row)
        by_source.append(row)
    tiles = jnp.concatenate(by_source, axis=0)
    kind = jnp.concatenate([kind] * NZ, axis=0)
    live = tiles > 0
    ones = live.astype(jnp.float32)
    dot = lambda x, y: jnp.dot(x, y, preferred_element_type=jnp.float32)
    per_row = dot(ones, same[...])
    at = dot(ones, within[...]) + dot(lower[...], per_row)
    sums = dot(column[...], per_row)
    n = [sums[:, 6 * k:6 * k + 1] for k in range(NZ)]
    c1, c2, c3, c4 = (float(c) for c in USUAL)
    least = lambda x, y, t: jnp.minimum(
        jnp.minimum(jnp.full_like(x, c4), c3 - x), jnp.minimum(c2 - x - y, c1 - x - y - t)
    )
    room_up, room_down = least(n[3], n[2], n[1]), least(n[5], n[6], n[7])
    four_up = jnp.clip(room_up, 0.0, n[4])
    four_down = n[4] - four_up
    short = (room_up < 0) | (room_down < 0) | (four_down > room_down)
    over[...] = jnp.broadcast_to(jnp.max(short.astype(jnp.float32), axis=0, keepdims=True), (1, 128)).astype(jnp.int32)
    up = (kind < 4) | ((kind == 4) & (at < four_up))
    base = jnp.zeros_like(at)
    for k, first in (
        (3, four_up), (2, four_up + n[3]), (1, four_up + n[3] + n[2]),
        (5, four_down), (6, four_down + n[5]), (7, four_down + n[5] + n[6]),
    ):
        base = jnp.where(kind == k, first, base)
    base = jnp.where((kind == 4) & (at >= four_up), -four_up, base)
    at = at + base

    places = lax.broadcasted_iota(jnp.int32, (128, 128), 0).astype(jnp.float32)
    found = []
    for way in range(2):
        mine_too = live[0:NW] & (up[0:NW] if way == 0 else ~up[0:NW]) & (kind[0:NW] > 0)
        place = jnp.where(mine_too, at[0:NW], -1.0)
        value = jnp.where(mine_too, tiles[0:NW], 0).astype(jnp.float32)
        total = jnp.zeros((128, 128), jnp.float32)
        for i in range(NW):
            total = jnp.where(place[i:i + 1] == places, value[i:i + 1], total)
        found.append(
            lax.dot_general(
                jnp.ones((8, 128), jnp.float32), total, (((1,), (1,)), ((), ())), preferred_element_type=jnp.float32
            )
        )
    row = lax.broadcasted_iota(jnp.int32, (8, 128), 0)
    src[...] = jnp.maximum(jnp.where(row == 0, found[0], found[1]).astype(jnp.int32) - 1, 0)

    cap = jnp.full((NZ * NW, 128), c1)
    for k in range(2, 7):
        cap = jnp.where(kind == k, (c1, c2, c3, c4)[min(k, NZ - k) - 1], cap)
    spot = jnp.clip(at, 0.0, cap - 1) + jnp.where(up, 0.0, cap)
    spot = spot.astype(jnp.int32)
    mine_at = jnp.maximum(tiles[0:NW] - 1, 0)
    for k in range(1, NZ):
        i = NZ - k
        mine_at = jnp.where(kind[0:NW] == k, spot[i * NW:(i + 1) * NW], mine_at)
    post[...] = mine_at
    keys_over.wait()


def exchange_requests(mine, k_own):
    vmem, anywhere = pl.BlockSpec(memory_space=pltpu.VMEM), pl.BlockSpec(memory_space=pl.ANY)
    lane, row = np.arange(128), np.arange(NZ * NW)
    block = (lane[:, None] // 6 == lane[None, :] // 6) & (lane[:, None] < 48)
    plane = row[:, None] // NW == row[None, :] // NW
    kinds = np.broadcast_to(np.where(lane < 48, lane // 6, 9), (NW, 128)).astype(np.int32)
    within = (block & (lane[:, None] < lane[None, :])).astype(np.float32)
    lower = (plane & (row[None, :] < row[:, None])).astype(np.float32)
    ints = lambda *shape: jax.ShapeDtypeStruct(shape, jnp.int32)
    return pl.pallas_call(
        requests_kernel,
        out_shape=(
            ints(NZ, NW, 128), ints(8, 128), ints(NW, 128), ints(1, 128),
            jax.ShapeDtypeStruct(k_own.shape, k_own.dtype),
        ),
        in_specs=[*[vmem] * 6, anywhere],
        out_specs=(*[vmem] * 4, anywhere),
        scratch_shapes=[
            pltpu.VMEM((NW, 1, 128), jnp.int32),
            pltpu.SemaphoreType.DMA,
            pltpu.SemaphoreType.DMA((16,)),
            pltpu.SemaphoreType.DMA((16,)),
        ],
        compiler_params=pltpu.CompilerParams(collective_id=0, has_side_effects=True),
        name="requests",
    )(mine, kinds, within, block.astype(np.float32), lower, plane.astype(np.float32), k_own)


def tiles_kernel(caps, arrays, fetch, src, post, over, *refs):
    cuts = (0, *caps[::-1])
    refs = list(refs)
    take = lambda n: [refs.pop(0) for _ in range(n)]
    owns = take(arrays)
    twins = [None if f else refs.pop(0) for f in fetch]
    outs, over_out = take(arrays), refs.pop(0)
    tab, lists, stage = take(arrays), take(arrays), take(arrays)
    hops = [take(STEPS) for _ in range(arrays)]
    overs, tab_sem, twin_send, z_send, z_recv, y_send, y_recv, y_local, over_send, over_recv = refs
    me = lax.axis_index("ctx")
    z, w = me // NW, me % NW
    core = me % 2
    twin_at = me + 1 - 2 * core
    towards = (((z + 1) % NZ) * NW + w, ((z + NZ - 1) % NZ) * NW + w)

    barrier = pltpu.get_barrier_semaphore()
    for other in towards:
        pl.semaphore_signal(barrier, inc=1, device_id=at_ctx(other), device_id_type=MESH)
    for r in range(1, NW):
        pl.semaphore_signal(barrier, inc=1, device_id=at_ctx(z * NW + (w + r) % NW), device_id_type=MESH)
    pl.semaphore_wait(barrier, NW + 1)

    loads = []
    for a in range(arrays):
        mine = tab[a].at[pl.ds(core * 128, 128)]
        pair = [pltpu.make_async_copy(owns[a], mine, tab_sem.at[a, 0])]
        if fetch[a]:
            pair.append(
                pltpu.make_async_remote_copy(
                    src_ref=owns[a], dst_ref=mine, send_sem=twin_send.at[a], recv_sem=tab_sem.at[a, 1],
                    device_id=at_ctx(twin_at), device_id_type=MESH,
                )
            )
        else:
            pair.append(
                pltpu.make_async_copy(twins[a], tab[a].at[pl.ds((1 - core) * 128, 128)], tab_sem.at[a, 1])
            )
        for copy in pair:
            copy.start()
        loads.append(pair)
    told = []
    for r in range(1, NW):
        copy = pltpu.make_async_remote_copy(
            src_ref=over, dst_ref=overs.at[r], send_sem=over_send.at[r], recv_sem=over_recv.at[r],
            device_id=at_ctx(z * NW + (w + r) % NW), device_id_type=MESH,
        )
        copy.start()
        told.append(copy)

    def hop(a, d, step, piece):
        lo, hi = cuts[piece], cuts[piece + 1]
        source = lists[a] if step == 1 else hops[a][step - 2]
        number = (0, 4, 7, 9)[step - 1] + piece
        return pltpu.make_async_remote_copy(
            src_ref=source.at[pl.ds(d * caps[max(step - 2, 0)] + lo, hi - lo)],
            dst_ref=hops[a][step - 1].at[pl.ds(d * caps[step - 1] + lo, hi - lo)],
            send_sem=z_send.at[a, d, number],
            recv_sem=z_recv.at[a, d, number],
            device_id=at_ctx(towards[d]),
            device_id_type=MESH,
        )

    def pack(a, piece):
        for d in range(2):
            def one(i, carry):
                lists[a][d * caps[0] + i] = tab[a][src[d, i]]
                return carry

            lax.fori_loop(cuts[piece], cuts[piece + 1], one, 0)

    def deliver(a, k):
        base = k * NW * 6
        source = tab[a] if k == 0 else hops[a][min(k, NZ - k) - 1]

        def one(i, carry):
            for j in range(6):
                stage[a][base + i * 6 + j] = source[post[i, k * 6 + j]]
            return carry

        lax.fori_loop(0, NW, one, 0)

        def send(r, carry):
            ow = (w + r) % NW
            pltpu.make_async_remote_copy(
                src_ref=stage[a].at[pl.ds(base + ow * 6, 6)],
                dst_ref=outs[a].at[pl.ds(base + w * 6, 6)],
                send_sem=y_send.at[a],
                recv_sem=y_recv.at[a],
                device_id=at_ctx(z * NW + ow),
                device_id_type=MESH,
            ).start()
            return carry

        lax.fori_loop(1, NW, send, 0)
        pltpu.make_async_copy(
            stage[a].at[pl.ds(base + w * 6, 6)], outs[a].at[pl.ds(base + w * 6, 6)], y_local.at[a]
        ).start()

    def arrive_and_pass(a, step):
        for piece in range(5 - step):
            for d in range(2):
                hop(a, d, step, piece).wait_recv()
                if piece < 4 - step:
                    hop(a, d, step + 1, piece).start()

    def start_first(a):
        for piece in range(STEPS):
            for d in range(2):
                hop(a, d, 1, piece).start()

    for copy in loads[0]:
        copy.wait()
    for piece in range(STEPS):
        pack(0, piece)
        for d in range(2):
            hop(0, d, 1, piece).start()
    if arrays == 2:
        for copy in loads[1]:
            copy.wait()
        for piece in range(STEPS):
            pack(1, piece)
    deliver(0, 0)
    arrive_and_pass(0, 1)
    if arrays == 2:
        start_first(1)
        deliver(1, 0)
    for a in range(arrays):
        if a:
            arrive_and_pass(a, 1)
        for step in range(1, STEPS):
            deliver(a, step)
            deliver(a, NZ - step)
            arrive_and_pass(a, step + 1)
        deliver(a, STEPS)
    for a in range(arrays):
        for d in range(2):
            for step in range(1, STEPS + 1):
                for piece in range(STEPS + 1 - step):
                    hop(a, d, step, piece).wait_send()
    most = over[...]
    for r, copy in enumerate(told):
        copy.wait()
        most = jnp.maximum(most, overs[r + 1])
    over_out[...] = most
    remote, local = NZ * (NW - 1) * 6, NZ * 6
    for a in range(arrays):
        pltpu.make_async_copy(stage[a].at[pl.ds(0, remote)], stage[a].at[pl.ds(0, remote)], y_send.at[a]).wait()
        pltpu.make_async_copy(outs[a].at[pl.ds(0, remote)], outs[a].at[pl.ds(0, remote)], y_recv.at[a]).wait()
        pltpu.make_async_copy(outs[a].at[pl.ds(0, local)], outs[a].at[pl.ds(0, local)], y_local.at[a]).wait()


def exchange_tiles(number, caps, src, post, over, owns, twins):
    n = len(owns)
    fetch = tuple(t is None for t in twins)
    given = [t for t in twins if t is not None]
    tiles = jax.ShapeDtypeStruct((NZ * NW * 6, BLK, HD), owns[0].dtype)
    vmem = lambda *shape: pltpu.VMEM((*shape, BLK, HD), jnp.bfloat16)
    smem, whole = pl.BlockSpec(memory_space=pltpu.SMEM), pl.BlockSpec(memory_space=pltpu.VMEM)
    anywhere = pl.BlockSpec(memory_space=pl.ANY)
    dma = pltpu.SemaphoreType.DMA
    return pl.pallas_call(
        lambda *refs: tiles_kernel(caps, n, fetch, *refs),
        out_shape=(*[tiles] * n, jax.ShapeDtypeStruct((1, 128), jnp.int32)),
        in_specs=[smem, smem, whole, *[anywhere] * (n + len(given))],
        out_specs=(*[anywhere] * n, whole),
        scratch_shapes=[
            *[vmem(256)] * n,
            *[vmem(2 * caps[0])] * n,
            *[vmem(NZ * NW * 6)] * n,
            *[vmem(2 * c) for c in caps] * n,
            pltpu.VMEM((NW, 1, 128), jnp.int32),
            dma((n, 2)), dma((n,)), dma((n, 2, 10)), dma((n, 2, 10)),
            dma((n,)), dma((n,)), dma((n,)), dma((NW,)), dma((NW,)),
        ],
        compiler_params=pltpu.CompilerParams(
            collective_id=number, has_side_effects=True, vmem_limit_bytes=60 * 2**20
        ),
        name="tiles",
    )(src, post, over, *owns, *given)


def attend_kernel(where, counts, over, q, k, v, out, over_out, merged, qf, kc, vc, overs, send_sem, recv_sem, own_sem, over_send, over_recv):
    me = lax.axis_index("head")
    barrier = pltpu.get_barrier_semaphore()
    for r in range(1, 4):
        pl.semaphore_signal(barrier, inc=1, device_id={"head": (me + r) % 4}, device_id_type=MESH)
    pl.semaphore_wait(barrier, 3)
    told = []
    for r in range(1, 4):
        copy = pltpu.make_async_remote_copy(
            src_ref=over, dst_ref=overs.at[r], send_sem=over_send.at[r], recv_sem=over_recv.at[r],
            device_id={"head": (me + r) % 4}, device_id_type=MESH,
        )
        copy.start()
        told.append(copy)
    keys = SEL * BLK
    factor = float(HD ** -0.5 * np.log2(np.e))
    vc[:, HD:] = jnp.ones((keys, HD), jnp.bfloat16)
    first = ((me + 1) * 3 // 2) % 6

    def one_block(i, carry):
        b = (first + i) % 6
        qf[...] = q[pl.ds(b * BLK, BLK)].astype(jnp.float32).reshape(BLK * 16, HD)
        for g in range(2):
            item = b * 2 + g

            def gather(s, c):
                at = where[item * SEL + s]
                kc[pl.ds(s * BLK, BLK)] = k[at]
                vc[pl.ds(s * BLK, BLK), 0:HD] = v[at]
                return c

            lax.fori_loop(0, SEL, gather, 0)
            rows = jnp.concatenate(
                [qf[pl.ds(g * 8 + h, BLK, stride=16)].astype(jnp.bfloat16) for h in range(8)], axis=0
            )
            s = lax.dot_general(rows, kc[...], (((1,), (1,)), ((), ())), preferred_element_type=jnp.float32)
            kept = lax.broadcasted_iota(jnp.int32, (1, keys), 1) < counts[item] * BLK
            s = jnp.where(kept, s, -jnp.inf)
            top = jnp.max(s, axis=1, keepdims=True)
            p = jnp.exp2((s - top) * factor).astype(jnp.bfloat16)
            o = jnp.dot(p, vc[...], preferred_element_type=jnp.float32)
            o = o[:, 0:HD] / o[:, HD:]
            for h in range(8):
                merged[pl.ds(b * BLK, BLK), pl.ds(g * 1024 + h * HD, HD)] = o[h * BLK:(h + 1) * BLK].astype(jnp.bfloat16)
        for half in range(2):
            unit = b * 2 + half
            to = unit // 3
            source = merged.at[pl.ds(unit * 32, 32)]
            target = out.at[pl.ds((unit % 3) * 32, 32), pl.ds(pl.multiple_of(me * 2048, 2048), 2048)]

            @pl.when(to == me)
            def _():
                pltpu.make_async_copy(source, target, own_sem).start()

            @pl.when(to != me)
            def _():
                pltpu.make_async_remote_copy(
                    src_ref=source, dst_ref=target, send_sem=send_sem, recv_sem=recv_sem,
                    device_id={"head": to}, device_id_type=MESH,
                ).start()
        return carry

    lax.fori_loop(0, 6, one_block, 0)
    most = over[...]
    for r, copy in enumerate(told):
        copy.wait()
        most = jnp.maximum(most, overs[r + 1])
    over_out[...] = most
    pltpu.make_async_copy(out.at[:, pl.ds(0, 2048)], out.at[:, pl.ds(0, 2048)], own_sem).wait()
    pltpu.make_async_copy(out.at[:, pl.ds(0, 6144)], out.at[:, pl.ds(0, 6144)], send_sem).wait()
    pltpu.make_async_copy(out.at[:, pl.ds(0, 6144)], out.at[:, pl.ds(0, 6144)], recv_sem).wait()


def attend_all(number, where, counts, over, queries, k, v):
    smem, vmem = pl.BlockSpec(memory_space=pltpu.SMEM), pl.BlockSpec(memory_space=pltpu.VMEM)
    dma = pltpu.SemaphoreType.DMA
    return pl.pallas_call(
        attend_kernel,
        out_shape=(jax.ShapeDtypeStruct((96, 8192), jnp.bfloat16), jax.ShapeDtypeStruct((1, 128), jnp.int32)),
        in_specs=[smem, smem, vmem, vmem, vmem, vmem],
        out_specs=(pl.BlockSpec(memory_space=pl.ANY), vmem),
        scratch_shapes=[
            pltpu.VMEM((384, 2048), jnp.bfloat16),
            pltpu.VMEM((BLK * 16, HD), jnp.float32),
            pltpu.VMEM((SEL * BLK, HD), jnp.bfloat16),
            pltpu.VMEM((SEL * BLK, 2 * HD), jnp.bfloat16),
            pltpu.VMEM((4, 1, 128), jnp.int32),
            dma, dma, dma, dma((4,)), dma((4,)),
        ],
        compiler_params=pltpu.CompilerParams(
            collective_id=number, has_side_effects=True, vmem_limit_bytes=60 * 2**20
        ),
        name="attend",
    )(where, counts, over, queries, k, v)


def own_requests(blocks, counts):
    me = lax.axis_index("ctx")
    z = me // NW
    flat = blocks.reshape(-1)
    ids = np.arange(ITEMS * SEL)
    live = (jnp.asarray(ids % SEL)[None, :].reshape(ITEMS, SEL) < counts.reshape(ITEMS, 1)).reshape(-1)
    holder = jnp.where(live, flat // BLK, -1)
    earlier = jnp.asarray(ids[None, :] < ids[:, None])
    rank = jnp.sum(((holder[:, None] == holder[None, :]) & earlier).astype(jnp.int32), axis=1)
    core = holder % 2
    lane = (holder // 2 % 4) * 2 + (rank + core) % 2
    away = (z - holder // NW + NZ) % NZ
    inside = core * 3 + rank // 2
    tile = core * 128 + jnp.asarray(ids // SEL % 2) * BLK + flat % BLK + 1
    slot = jnp.where(live, lane * 48 + away * 6 + inside, -1)
    mine = jnp.sum(jnp.where(slot[None, :] == jnp.arange(NW * 48)[:, None], tile[None, :], 0), axis=1)
    mine = jnp.pad(mine.reshape(NW, 1, 48), ((0, 0), (0, 0), (0, 80)))
    where = jnp.where(live, away * 48 + lane * 6 + inside, 0)
    return mine, where


def full_plan(table):
    asked = table[:, :, :48].reshape(NZ, NW, NZ, 6)
    by_k = [jnp.roll(asked[:, :, k], -k, axis=0) for k in range(NZ)]
    up = [by_k[4][:, 0::2], by_k[3], by_k[2], by_k[1]]
    down = [by_k[4][:, 1::2], by_k[5], by_k[6], by_k[7]]
    lists = jnp.stack([jnp.concatenate([e.reshape(NZ, -1) for e in way], axis=1) for way in (up, down)])
    live = lists > 0
    size = lists.shape[2]
    before = jnp.asarray(np.triu(np.ones((size, size), np.float32), 1))
    at = jnp.dot(live.reshape(-1, size).astype(jnp.float32), before).astype(jnp.int32).reshape(lists.shape)
    hit = (at[:, 0, None, :] == jnp.arange(size)[None, :, None]) & live[:, 0, None, :]
    src = jnp.maximum(jnp.sum(jnp.where(hit, lists[:, 0, None, :], 0), axis=2) - 1, 0)

    def seg(d, k, part):
        lo, hi = (0, 24) if part == 0 else (24 + 48 * (part - 1), 24 + 48 * part)
        return jnp.minimum(at[d, (NZ - k) % NZ, lo:hi], FULL[3 - part] - 1) + d * FULL[3 - part]

    here = jnp.maximum(by_k[0][0] - 1, 0)
    four = jnp.stack([seg(0, 4, 0).reshape(4, 6), seg(1, 4, 0).reshape(4, 6)], axis=1)
    parts = [here, seg(0, 1, 3), seg(0, 2, 2), seg(0, 3, 1), four, seg(1, 5, 1), seg(1, 6, 2), seg(1, 7, 3)]
    return src, jnp.concatenate([p.reshape(NW, 6) for p in parts], axis=1)


def per_device(queries, keys, values, sel_blocks, sel_counts):
    k_own = keys.reshape(128, BLK, HD)
    v_own = values.reshape(128, BLK, HD)
    mine, where = own_requests(sel_blocks, sel_counts)
    counts = sel_counts.reshape(-1)
    table, src, post, over, k_twin = exchange_requests(mine, k_own)
    k, v, over = exchange_tiles(1, USUAL, src, post, over, (k_own, v_own), (k_twin, None))
    out, over = attend_all(2, where, counts, over, queries, k, v)

    def again():
        src, post = full_plan(table)
        none = jnp.zeros((1, 128), jnp.int32)
        k, _ = exchange_tiles(3, FULL, src, post, none, (k_own,), (None,))
        v, _ = exchange_tiles(4, FULL, src, post, none, (v_own,), (None,))
        return attend_all(5, where, counts, none, queries, k, v)[0]

    return lax.cond(over[0, 0] > 0, again, lambda: out)


def solution(mesh):
    placed = (
        P("ctx", "head", None),
        P("head", "ctx", None),
        P("head", "ctx", None),
        P("ctx", "head", None),
        P("ctx", "head"),
    )
    return jax.shard_map(
        per_device, mesh=mesh, in_specs=placed, out_specs=P(("ctx", "head"), None), check_vma=False
    )
```

```python
import jax
import jax.numpy as jnp
import numpy as np
from jax import lax
from jax.experimental import pallas as pl
from jax.experimental.pallas import tpu as pltpu
from jax.sharding import PartitionSpec as P

BLK = 64
HD = 128
SEL = 16
ITEMS = 12
NZ = 8
NW = 8
STEPS = 4
USUAL = (104, 78, 50, 24)
FULL = (168, 120, 72, 24)
MESH = pl.DeviceIdType.MESH


def at_ctx(index):
    return {"ctx": index}


def requests_kernel(
    mine, kinds, within, same, lower, column, k_own,
    table, src, post, over, k_twin,
    rows, local_sem, send_sem, recv_sem,
):
    me = lax.axis_index("ctx")
    z, w = me // NW, me % NW
    barrier = pltpu.get_barrier_semaphore()
    for r in range(1, 8):
        pl.semaphore_signal(barrier, inc=1, device_id=at_ctx(z * NW + (w + r) % NW), device_id_type=MESH)
        pl.semaphore_signal(barrier, inc=1, device_id=at_ctx((z + r) % NZ * NW + w), device_id_type=MESH)
    pl.semaphore_wait(barrier, 14)

    own = pltpu.make_async_copy(mine.at[pl.ds(w, 1)], rows.at[pl.ds(w, 1)], local_sem)
    own.start()
    inside = []
    for r in range(1, NW):
        ow = (w + r) % NW
        copy = pltpu.make_async_remote_copy(
            src_ref=mine.at[pl.ds(ow, 1)], dst_ref=rows.at[pl.ds(w, 1)],
            send_sem=send_sem.at[r], recv_sem=recv_sem.at[r],
            device_id=at_ctx(z * NW + ow), device_id_type=MESH,
        )
        copy.start()
        inside.append(copy)
    keys_over = pltpu.make_async_remote_copy(
        src_ref=k_own, dst_ref=k_twin, send_sem=send_sem.at[0], recv_sem=recv_sem.at[0],
        device_id=at_ctx(me + 1 - 2 * (me % 2)), device_id_type=MESH,
    )
    keys_over.start()
    own.wait()
    for copy in inside:
        copy.wait()
    table[0] = jnp.concatenate([rows[i] for i in range(NW)], axis=0)
    along = []
    for r in range(1, NZ):
        copy = pltpu.make_async_remote_copy(
            src_ref=table.at[0], dst_ref=table.at[NZ - r],
            send_sem=send_sem.at[NW + r], recv_sem=recv_sem.at[NW + r],
            device_id=at_ctx((z + r) % NZ * NW + w), device_id_type=MESH,
        )
        copy.start()
        along.append(copy)
    for copy in along:
        copy.wait()

    kind = kinds[...]
    asked = [table[i] for i in range(NZ)]
    by_source = []
    for i in range(NZ):
        row = jnp.zeros((NW, 128), jnp.int32)
        for k in range(NZ):
            row = jnp.where(kind == k, asked[(i + k) % NZ], row)
        by_source.append(row)
    tiles = jnp.concatenate(by_source, axis=0)
    kind = jnp.concatenate([kind] * NZ, axis=0)
    live = tiles > 0
    ones = live.astype(jnp.float32)
    dot = lambda x, y: jnp.dot(x, y, preferred_element_type=jnp.float32)
    per_row = dot(ones, same[...])
    at = dot(ones, within[...]) + dot(lower[...], per_row)
    sums = dot(column[...], per_row)
    n = [sums[:, 6 * k:6 * k + 1] for k in range(NZ)]
    c1, c2, c3, c4 = (float(c) for c in USUAL)
    least = lambda x, y, t: jnp.minimum(
        jnp.minimum(jnp.full_like(x, c4), c3 - x), jnp.minimum(c2 - x - y, c1 - x - y - t)
    )
    room_up, room_down = least(n[3], n[2], n[1]), least(n[5], n[6], n[7])
    four_up = jnp.clip(room_up, 0.0, n[4])
    four_down = n[4] - four_up
    short = (room_up < 0) | (room_down < 0) | (four_down > room_down)
    over[...] = jnp.broadcast_to(jnp.max(short.astype(jnp.float32), axis=0, keepdims=True), (1, 128)).astype(jnp.int32)
    up = (kind < 4) | ((kind == 4) & (at < four_up))
    base = jnp.zeros_like(at)
    for k, first in (
        (3, four_up), (2, four_up + n[3]), (1, four_up + n[3] + n[2]),
        (5, four_down), (6, four_down + n[5]), (7, four_down + n[5] + n[6]),
    ):
        base = jnp.where(kind == k, first, base)
    base = jnp.where((kind == 4) & (at >= four_up), -four_up, base)
    at = at + base

    places = lax.broadcasted_iota(jnp.int32, (128, 128), 0).astype(jnp.float32)
    found = []
    for way in range(2):
        mine_too = live[0:NW] & (up[0:NW] if way == 0 else ~up[0:NW]) & (kind[0:NW] > 0)
        place = jnp.where(mine_too, at[0:NW], -1.0)
        value = jnp.where(mine_too, tiles[0:NW], 0).astype(jnp.float32)
        total = jnp.zeros((128, 128), jnp.float32)
        for i in range(NW):
            total = jnp.where(place[i:i + 1] == places, value[i:i + 1], total)
        found.append(
            lax.dot_general(
                jnp.ones((8, 128), jnp.float32), total, (((1,), (1,)), ((), ())), preferred_element_type=jnp.float32
            )
        )
    row = lax.broadcasted_iota(jnp.int32, (8, 128), 0)
    src[...] = jnp.maximum(jnp.where(row == 0, found[0], found[1]).astype(jnp.int32) - 1, 0)

    cap = jnp.full((NZ * NW, 128), c1)
    for k in range(2, 7):
        cap = jnp.where(kind == k, (c1, c2, c3, c4)[min(k, NZ - k) - 1], cap)
    spot = jnp.clip(at, 0.0, cap - 1) + jnp.where(up, 0.0, cap)
    spot = spot.astype(jnp.int32)
    mine_at = jnp.maximum(tiles[0:NW] - 1, 0)
    for k in range(1, NZ):
        i = NZ - k
        mine_at = jnp.where(kind[0:NW] == k, spot[i * NW:(i + 1) * NW], mine_at)
    post[...] = mine_at
    keys_over.wait()


def exchange_requests(mine, k_own):
    vmem, anywhere = pl.BlockSpec(memory_space=pltpu.VMEM), pl.BlockSpec(memory_space=pl.ANY)
    lane, row = np.arange(128), np.arange(NZ * NW)
    block = (lane[:, None] // 6 == lane[None, :] // 6) & (lane[:, None] < 48)
    plane = row[:, None] // NW == row[None, :] // NW
    kinds = np.broadcast_to(np.where(lane < 48, lane // 6, 9), (NW, 128)).astype(np.int32)
    within = (block & (lane[:, None] < lane[None, :])).astype(np.float32)
    lower = (plane & (row[None, :] < row[:, None])).astype(np.float32)
    ints = lambda *shape: jax.ShapeDtypeStruct(shape, jnp.int32)
    return pl.pallas_call(
        requests_kernel,
        out_shape=(
            ints(NZ, NW, 128), ints(8, 128), ints(NW, 128), ints(1, 128),
            jax.ShapeDtypeStruct(k_own.shape, k_own.dtype),
        ),
        in_specs=[*[vmem] * 6, anywhere],
        out_specs=(*[vmem] * 4, anywhere),
        scratch_shapes=[
            pltpu.VMEM((NW, 1, 128), jnp.int32),
            pltpu.SemaphoreType.DMA,
            pltpu.SemaphoreType.DMA((16,)),
            pltpu.SemaphoreType.DMA((16,)),
        ],
        compiler_params=pltpu.CompilerParams(collective_id=0, has_side_effects=True),
        name="requests",
    )(mine, kinds, within, block.astype(np.float32), lower, plane.astype(np.float32), k_own)


def tiles_kernel(caps, arrays, fetch, src, post, over, *refs):
    cuts = (0, *caps[::-1])
    refs = list(refs)
    take = lambda n: [refs.pop(0) for _ in range(n)]
    owns = take(arrays)
    twins = [None if f else refs.pop(0) for f in fetch]
    outs, over_out = take(arrays), refs.pop(0)
    tab, lists, stage = take(arrays), take(arrays), take(arrays)
    hops = [take(STEPS) for _ in range(arrays)]
    overs, tab_sem, twin_send, z_send, z_recv, y_send, y_recv, y_local, over_send, over_recv = refs
    me = lax.axis_index("ctx")
    z, w = me // NW, me % NW
    core = me % 2
    twin_at = me + 1 - 2 * core
    towards = (((z + 1) % NZ) * NW + w, ((z + NZ - 1) % NZ) * NW + w)

    barrier = pltpu.get_barrier_semaphore()
    for other in towards:
        pl.semaphore_signal(barrier, inc=1, device_id=at_ctx(other), device_id_type=MESH)
    for r in range(1, NW):
        pl.semaphore_signal(barrier, inc=1, device_id=at_ctx(z * NW + (w + r) % NW), device_id_type=MESH)
    pl.semaphore_wait(barrier, NW + 1)

    loads = []
    for a in range(arrays):
        mine = tab[a].at[pl.ds(core * 128, 128)]
        pair = [pltpu.make_async_copy(owns[a], mine, tab_sem.at[a, 0])]
        if fetch[a]:
            pair.append(
                pltpu.make_async_remote_copy(
                    src_ref=owns[a], dst_ref=mine, send_sem=twin_send.at[a], recv_sem=tab_sem.at[a, 1],
                    device_id=at_ctx(twin_at), device_id_type=MESH,
                )
            )
        else:
            pair.append(
                pltpu.make_async_copy(twins[a], tab[a].at[pl.ds((1 - core) * 128, 128)], tab_sem.at[a, 1])
            )
        for copy in pair:
            copy.start()
        loads.append(pair)
    told = []
    for r in range(1, NW):
        copy = pltpu.make_async_remote_copy(
            src_ref=over, dst_ref=overs.at[r], send_sem=over_send.at[r], recv_sem=over_recv.at[r],
            device_id=at_ctx(z * NW + (w + r) % NW), device_id_type=MESH,
        )
        copy.start()
        told.append(copy)

    def hop(a, d, step, piece):
        lo, hi = cuts[piece], cuts[piece + 1]
        source = lists[a] if step == 1 else hops[a][step - 2]
        number = (0, 4, 7, 9)[step - 1] + piece
        return pltpu.make_async_remote_copy(
            src_ref=source.at[pl.ds(d * caps[max(step - 2, 0)] + lo, hi - lo)],
            dst_ref=hops[a][step - 1].at[pl.ds(d * caps[step - 1] + lo, hi - lo)],
            send_sem=z_send.at[a, d, number],
            recv_sem=z_recv.at[a, d, number],
            device_id=at_ctx(towards[d]),
            device_id_type=MESH,
        )

    def pack(a, piece):
        for d in range(2):
            def one(i, carry):
                lists[a][d * caps[0] + i] = tab[a][src[d, i]]
                return carry

            lax.fori_loop(cuts[piece], cuts[piece + 1], one, 0)

    def deliver(a, k):
        base = k * NW * 6
        source = tab[a] if k == 0 else hops[a][min(k, NZ - k) - 1]

        def one(i, carry):
            for j in range(6):
                stage[a][base + i * 6 + j] = source[post[i, k * 6 + j]]
            return carry

        lax.fori_loop(0, NW, one, 0)

        def send(r, carry):
            ow = (w + r) % NW
            pltpu.make_async_remote_copy(
                src_ref=stage[a].at[pl.ds(base + ow * 6, 6)],
                dst_ref=outs[a].at[pl.ds(base + w * 6, 6)],
                send_sem=y_send.at[a],
                recv_sem=y_recv.at[a],
                device_id=at_ctx(z * NW + ow),
                device_id_type=MESH,
            ).start()
            return carry

        lax.fori_loop(1, NW, send, 0)
        pltpu.make_async_copy(
            stage[a].at[pl.ds(base + w * 6, 6)], outs[a].at[pl.ds(base + w * 6, 6)], y_local.at[a]
        ).start()

    def arrive_and_pass(a, step):
        for piece in range(5 - step):
            for d in range(2):
                hop(a, d, step, piece).wait_recv()
                if piece < 4 - step:
                    hop(a, d, step + 1, piece).start()

    def start_first(a):
        for piece in range(STEPS):
            for d in range(2):
                hop(a, d, 1, piece).start()

    for copy in loads[0]:
        copy.wait()
    for piece in range(STEPS):
        pack(0, piece)
        for d in range(2):
            hop(0, d, 1, piece).start()
    if arrays == 2:
        for copy in loads[1]:
            copy.wait()
        for piece in range(STEPS):
            pack(1, piece)
    deliver(0, 0)
    arrive_and_pass(0, 1)
    if arrays == 2:
        start_first(1)
        deliver(1, 0)
    for a in range(arrays):
        if a:
            arrive_and_pass(a, 1)
        for step in range(1, STEPS):
            deliver(a, step)
            deliver(a, NZ - step)
            arrive_and_pass(a, step + 1)
        deliver(a, STEPS)
    for a in range(arrays):
        for d in range(2):
            for step in range(1, STEPS + 1):
                for piece in range(STEPS + 1 - step):
                    hop(a, d, step, piece).wait_send()
    most = over[...]
    for r, copy in enumerate(told):
        copy.wait()
        most = jnp.maximum(most, overs[r + 1])
    over_out[...] = most
    remote, local = NZ * (NW - 1) * 6, NZ * 6
    for a in range(arrays):
        pltpu.make_async_copy(stage[a].at[pl.ds(0, remote)], stage[a].at[pl.ds(0, remote)], y_send.at[a]).wait()
        pltpu.make_async_copy(outs[a].at[pl.ds(0, remote)], outs[a].at[pl.ds(0, remote)], y_recv.at[a]).wait()
        pltpu.make_async_copy(outs[a].at[pl.ds(0, local)], outs[a].at[pl.ds(0, local)], y_local.at[a]).wait()


def exchange_tiles(number, caps, src, post, over, owns, twins):
    n = len(owns)
    fetch = tuple(t is None for t in twins)
    given = [t for t in twins if t is not None]
    tiles = jax.ShapeDtypeStruct((NZ * NW * 6, BLK, HD), owns[0].dtype)
    vmem = lambda *shape: pltpu.VMEM((*shape, BLK, HD), jnp.bfloat16)
    smem, whole = pl.BlockSpec(memory_space=pltpu.SMEM), pl.BlockSpec(memory_space=pltpu.VMEM)
    anywhere = pl.BlockSpec(memory_space=pl.ANY)
    dma = pltpu.SemaphoreType.DMA
    return pl.pallas_call(
        lambda *refs: tiles_kernel(caps, n, fetch, *refs),
        out_shape=(*[tiles] * n, jax.ShapeDtypeStruct((1, 128), jnp.int32)),
        in_specs=[smem, smem, whole, *[anywhere] * (n + len(given))],
        out_specs=(*[anywhere] * n, whole),
        scratch_shapes=[
            *[vmem(256)] * n,
            *[vmem(2 * caps[0])] * n,
            *[vmem(NZ * NW * 6)] * n,
            *[vmem(2 * c) for c in caps] * n,
            pltpu.VMEM((NW, 1, 128), jnp.int32),
            dma((n, 2)), dma((n,)), dma((n, 2, 10)), dma((n, 2, 10)),
            dma((n,)), dma((n,)), dma((n,)), dma((NW,)), dma((NW,)),
        ],
        compiler_params=pltpu.CompilerParams(
            collective_id=number, has_side_effects=True, vmem_limit_bytes=60 * 2**20
        ),
        name="tiles",
    )(src, post, over, *owns, *given)


def attend_kernel(where, counts, over, q, k, v, out, over_out, merged, qf, kc, vc, overs, send_sem, recv_sem, own_sem, over_send, over_recv):
    me = lax.axis_index("head")
    barrier = pltpu.get_barrier_semaphore()
    for r in range(1, 4):
        pl.semaphore_signal(barrier, inc=1, device_id={"head": (me + r) % 4}, device_id_type=MESH)
    pl.semaphore_wait(barrier, 3)
    told = []
    for r in range(1, 4):
        copy = pltpu.make_async_remote_copy(
            src_ref=over, dst_ref=overs.at[r], send_sem=over_send.at[r], recv_sem=over_recv.at[r],
            device_id={"head": (me + r) % 4}, device_id_type=MESH,
        )
        copy.start()
        told.append(copy)
    keys = SEL * BLK
    factor = float(HD ** -0.5 * np.log2(np.e))
    vc[:, HD:] = jnp.ones((keys, HD), jnp.bfloat16)
    first = ((me + 1) * 3 // 2) % 6

    def one_block(i, carry):
        b = (first + i) % 6
        qf[...] = q[pl.ds(b * BLK, BLK)].astype(jnp.float32).reshape(BLK * 16, HD)
        for g in range(2):
            item = b * 2 + g

            def gather(s, c):
                at = where[item * SEL + s]
                kc[pl.ds(s * BLK, BLK)] = k[at]
                vc[pl.ds(s * BLK, BLK), 0:HD] = v[at]
                return c

            lax.fori_loop(0, SEL, gather, 0)
            rows = jnp.concatenate(
                [qf[pl.ds(g * 8 + h, BLK, stride=16)].astype(jnp.bfloat16) for h in range(8)], axis=0
            )
            s = lax.dot_general(rows, kc[...], (((1,), (1,)), ((), ())), preferred_element_type=jnp.float32)
            kept = lax.broadcasted_iota(jnp.int32, (1, keys), 1) < counts[item] * BLK
            s = jnp.where(kept, s, -jnp.inf)
            top = jnp.max(s, axis=1, keepdims=True)
            p = jnp.exp2((s - top) * factor).astype(jnp.bfloat16)
            o = jnp.dot(p, vc[...], preferred_element_type=jnp.float32)
            o = o[:, 0:HD] / o[:, HD:]
            for h in range(8):
                merged[pl.ds(b * BLK, BLK), pl.ds(g * 1024 + h * HD, HD)] = o[h * BLK:(h + 1) * BLK].astype(jnp.bfloat16)
        for half in range(2):
            unit = b * 2 + half
            to = unit // 3
            source = merged.at[pl.ds(unit * 32, 32)]
            target = out.at[pl.ds((unit % 3) * 32, 32), pl.ds(pl.multiple_of(me * 2048, 2048), 2048)]

            @pl.when(to == me)
            def _():
                pltpu.make_async_copy(source, target, own_sem).start()

            @pl.when(to != me)
            def _():
                pltpu.make_async_remote_copy(
                    src_ref=source, dst_ref=target, send_sem=send_sem, recv_sem=recv_sem,
                    device_id={"head": to}, device_id_type=MESH,
                ).start()
        return carry

    lax.fori_loop(0, 6, one_block, 0)
    most = over[...]
    for r, copy in enumerate(told):
        copy.wait()
        most = jnp.maximum(most, overs[r + 1])
    over_out[...] = most
    pltpu.make_async_copy(out.at[:, pl.ds(0, 2048)], out.at[:, pl.ds(0, 2048)], own_sem).wait()
    pltpu.make_async_copy(out.at[:, pl.ds(0, 6144)], out.at[:, pl.ds(0, 6144)], send_sem).wait()
    pltpu.make_async_copy(out.at[:, pl.ds(0, 6144)], out.at[:, pl.ds(0, 6144)], recv_sem).wait()


def attend_all(number, where, counts, over, queries, k, v):
    smem, vmem = pl.BlockSpec(memory_space=pltpu.SMEM), pl.BlockSpec(memory_space=pltpu.VMEM)
    dma = pltpu.SemaphoreType.DMA
    return pl.pallas_call(
        attend_kernel,
        out_shape=(jax.ShapeDtypeStruct((96, 8192), jnp.bfloat16), jax.ShapeDtypeStruct((1, 128), jnp.int32)),
        in_specs=[smem, smem, vmem, vmem, vmem, vmem],
        out_specs=(pl.BlockSpec(memory_space=pl.ANY), vmem),
        scratch_shapes=[
            pltpu.VMEM((384, 2048), jnp.bfloat16),
            pltpu.VMEM((BLK * 16, HD), jnp.float32),
            pltpu.VMEM((SEL * BLK, HD), jnp.bfloat16),
            pltpu.VMEM((SEL * BLK, 2 * HD), jnp.bfloat16),
            pltpu.VMEM((4, 1, 128), jnp.int32),
            dma, dma, dma, dma((4,)), dma((4,)),
        ],
        compiler_params=pltpu.CompilerParams(
            collective_id=number, has_side_effects=True, vmem_limit_bytes=60 * 2**20
        ),
        name="attend",
    )(where, counts, over, queries, k, v)


def fused_kernel(
    src, post, where, counts, over, q_in, k_own, v_own, k_twin, out, over_out,
    tab_k, tab_v, packed, stage, k1, k2, k3, k4, v1, v2, v3, v4, land_k, land_v, more,
    q, merged, qf, kc, vc, overs, overs_head,
    q_sem, tab_sem, twin_send, z_send, z_recv, y_send, y_recv, y_local,
    over_send, over_recv, out_send, out_recv, out_own,
):
    caps = USUAL
    cuts = (0, *caps[::-1])
    tab, land, hops = (tab_k, tab_v), (land_k, land_v), ((k1, k2, k3, k4), (v1, v2, v3, v4))
    me = lax.axis_index("ctx")
    head = lax.axis_index("head")
    z, w = me // NW, me % NW
    core = me % 2
    towards = (((z + 1) % NZ) * NW + w, ((z + NZ - 1) % NZ) * NW + w)

    barrier = pltpu.get_barrier_semaphore()
    for other in towards:
        pl.semaphore_signal(barrier, inc=1, device_id=at_ctx(other), device_id_type=MESH)
    for r in range(1, NW):
        pl.semaphore_signal(barrier, inc=1, device_id=at_ctx(z * NW + (w + r) % NW), device_id_type=MESH)
    for r in range(1, 4):
        pl.semaphore_signal(barrier, inc=1, device_id={"head": (head + r) % 4}, device_id_type=MESH)
    pl.semaphore_wait(barrier, NW + 4)

    mine_k, mine_v = (t.at[pl.ds(core * 128, 128)] for t in tab)
    twin_k = tab_k.at[pl.ds((1 - core) * 128, 128)]
    loads = (
        (pltpu.make_async_copy(k_own, mine_k, tab_sem.at[0, 0]), pltpu.make_async_copy(k_twin, twin_k, tab_sem.at[0, 1])),
        (
            pltpu.make_async_copy(v_own, mine_v, tab_sem.at[1, 0]),
            pltpu.make_async_remote_copy(
                src_ref=v_own, dst_ref=mine_v, send_sem=twin_send, recv_sem=tab_sem.at[1, 1],
                device_id=at_ctx(me + 1 - 2 * core), device_id_type=MESH,
            ),
        ),
    )
    for pair in loads:
        for copy in pair:
            copy.start()
    q_load = pltpu.make_async_copy(q_in, q, q_sem)
    q_load.start()
    told = []
    for r in range(1, NW):
        copy = pltpu.make_async_remote_copy(
            src_ref=over, dst_ref=overs.at[r], send_sem=over_send.at[r], recv_sem=over_recv.at[r],
            device_id=at_ctx(z * NW + (w + r) % NW), device_id_type=MESH,
        )
        copy.start()
        told.append(copy)

    def hop(a, d, step, piece):
        lo, hi = cuts[piece], cuts[piece + 1]
        source = packed if step == 1 else hops[a][step - 2]
        number = (0, 4, 7, 9)[step - 1] + piece
        return pltpu.make_async_remote_copy(
            src_ref=source.at[pl.ds(d * caps[max(step - 2, 0)] + lo, hi - lo)],
            dst_ref=hops[a][step - 1].at[pl.ds(d * caps[step - 1] + lo, hi - lo)],
            send_sem=z_send.at[a, d, number],
            recv_sem=z_recv.at[a, d, number],
            device_id=at_ctx(towards[d]),
            device_id_type=MESH,
        )

    def pack_and_start(a):
        for piece in range(STEPS):
            for d in range(2):
                def one(i, carry):
                    packed[d * caps[0] + i] = tab[a][src[d, i]]
                    return carry

                lax.fori_loop(cuts[piece], cuts[piece + 1], one, 0)
                hop(a, d, 1, piece).start()

    def settle(a, k):
        pltpu.make_async_copy(stage.at[pl.ds(0, 42)], stage.at[pl.ds(0, 42)], y_send.at[a, k]).wait()
        pltpu.make_async_copy(stage.at[pl.ds(0, 6)], stage.at[pl.ds(0, 6)], y_local.at[a, k]).wait()

    def deliver(a, k):
        base = k * NW * 6
        source = tab[a] if k == 0 else hops[a][min(k, NZ - k) - 1]
        if a and k != STEPS:
            settle(0, k)

        def one(i, carry):
            for j in range(6):
                stage[base + i * 6 + j] = source[post[i, k * 6 + j]]
            return carry

        lax.fori_loop(0, NW, one, 0)

        def send(r, carry):
            ow = (w + r) % NW
            pltpu.make_async_remote_copy(
                src_ref=stage.at[pl.ds(base + ow * 6, 6)],
                dst_ref=land[a].at[pl.ds(base + w * 6, 6)],
                send_sem=y_send.at[a, k],
                recv_sem=y_recv.at[a],
                device_id=at_ctx(z * NW + ow),
                device_id_type=MESH,
            ).start()
            return carry

        lax.fori_loop(1, NW, send, 0)
        pltpu.make_async_copy(
            stage.at[pl.ds(base + w * 6, 6)], land[a].at[pl.ds(base + w * 6, 6)], y_local.at[a, k]
        ).start()

    def arrive_and_pass(a, step):
        for piece in range(5 - step):
            for d in range(2):
                hop(a, d, step, piece).wait_recv()
                if piece < 4 - step:
                    hop(a, d, step + 1, piece).start()

    def all_landed(a):
        remote = NZ * (NW - 1) * 6
        pltpu.make_async_copy(land[a].at[pl.ds(0, remote)], land[a].at[pl.ds(0, remote)], y_recv.at[a]).wait()

    keys = SEL * BLK
    factor = float(HD ** -0.5 * np.log2(np.e))
    first = ((head + 1) * 3 // 2) % 6 * 2

    def weigh(ref, n, spot):
        item = (first + n) % ITEMS
        b, g = item // 2, item % 2
        qf[...] = q[pl.ds(b * BLK, BLK)].astype(jnp.float32).reshape(BLK * 16, HD)

        def gather(i, c):
            kc[pl.ds(i * BLK, BLK)] = land_k[where[item * SEL + i]]
            return c

        lax.fori_loop(0, SEL, gather, 0)
        rows = jnp.concatenate(
            [qf[pl.ds(g * 8 + h, BLK, stride=16)].astype(jnp.bfloat16) for h in range(8)], axis=0
        )
        s = lax.dot_general(rows, kc[...], (((1,), (1,)), ((), ())), preferred_element_type=jnp.float32)
        kept = lax.broadcasted_iota(jnp.int32, (1, keys), 1) < counts[item] * BLK
        s = jnp.where(kept, s, -jnp.inf)
        top = jnp.max(s, axis=1, keepdims=True)
        p = jnp.exp2((s - top) * factor).astype(jnp.bfloat16)
        for h in range(8):
            for c in range(8):
                ref[spot * 64 + h * 8 + c] = p[h * BLK:(h + 1) * BLK, c * HD:(c + 1) * HD]

    def finish(ref, n, spot):
        item = (first + n) % ITEMS
        b, g = item // 2, item % 2

        def gather(i, c):
            vc[pl.ds(i * BLK, BLK), 0:HD] = land_v[where[item * SEL + i]]
            return c

        lax.fori_loop(0, SEL, gather, 0)
        p = jnp.concatenate(
            [jnp.concatenate([ref[spot * 64 + h * 8 + c] for c in range(8)], axis=1) for h in range(8)], axis=0
        )
        o = jnp.dot(p, vc[...], preferred_element_type=jnp.float32)
        o = (o[:, 0:HD] / o[:, HD:]).astype(jnp.bfloat16)
        for h in range(8):
            merged[pl.ds(b * BLK, BLK), pl.ds(pl.multiple_of(g * 1024 + h * HD, HD), HD)] = o[h * BLK:(h + 1) * BLK]

        @pl.when(g == 1)
        def _():
            for half in range(2):
                unit = b * 2 + half
                to = unit // 3
                source = merged.at[pl.ds(unit * 32, 32)]
                target = out.at[pl.ds((unit % 3) * 32, 32), pl.ds(pl.multiple_of(head * 2048, 2048), 2048)]

                @pl.when(to == head)
                def _():
                    pltpu.make_async_copy(source, target, out_own).start()

                @pl.when(to != head)
                def _():
                    pltpu.make_async_remote_copy(
                        src_ref=source, dst_ref=target, send_sem=out_send, recv_sem=out_recv,
                        device_id={"head": to}, device_id_type=MESH,
                    ).start()

    def over_items(work, ref, lo, hi):
        def one(n, carry):
            work(ref, n, n - lo)
            return carry

        lax.fori_loop(lo, hi, one, 0)

    for copy in loads[0]:
        copy.wait()
    pack_and_start(0)
    deliver(0, 0)
    arrive_and_pass(0, 1)
    for piece in range(STEPS):
        for d in range(2):
            hop(0, d, 1, piece).wait_send()
    for copy in loads[1]:
        copy.wait()
    pack_and_start(1)
    deliver(1, 0)
    deliver(0, 1)
    deliver(0, 7)
    arrive_and_pass(0, 2)
    deliver(0, 2)
    deliver(0, 6)
    arrive_and_pass(1, 1)
    deliver(1, 1)
    deliver(1, 7)
    arrive_and_pass(0, 3)
    deliver(0, 3)
    deliver(0, 5)
    arrive_and_pass(1, 2)
    deliver(1, 2)
    deliver(1, 6)
    arrive_and_pass(0, 4)
    deliver(0, 4)
    for step in range(2, STEPS + 1):
        for piece in range(STEPS + 1 - step):
            for d in range(2):
                hop(0, d, step, piece).wait_send()
    arrive_and_pass(1, 3)
    deliver(1, 3)
    deliver(1, 5)
    vc[:, HD:] = jnp.ones((keys, HD), jnp.bfloat16)
    q_load.wait()
    most = over[...]
    for r, copy in enumerate(told):
        copy.wait()
        most = jnp.maximum(most, overs[r + 1])
    overs_head[0] = most
    told = []
    for r in range(1, 4):
        copy = pltpu.make_async_remote_copy(
            src_ref=overs_head.at[0], dst_ref=overs_head.at[r], send_sem=over_send.at[NW + r], recv_sem=over_recv.at[NW + r],
            device_id={"head": (head + r) % 4}, device_id_type=MESH,
        )
        copy.start()
        told.append(copy)
    settle(0, STEPS)
    all_landed(0)
    over_items(weigh, tab_k, 0, 4)
    arrive_and_pass(1, 4)
    deliver(1, 4)
    over_items(weigh, k1, 4, 7)
    over_items(weigh, more, 7, ITEMS)
    for step in range(1, STEPS + 1):
        for piece in range(STEPS + 1 - step):
            for d in range(2):
                hop(1, d, step, piece).wait_send()
    for k in range(NZ):
        settle(1, k)
    all_landed(1)
    over_items(finish, tab_k, 0, 4)
    over_items(finish, k1, 4, 7)
    over_items(finish, more, 7, ITEMS)
    for r, copy in enumerate(told):
        copy.wait()
        most = jnp.maximum(most, overs_head[r + 1])
    over_out[...] = most
    pltpu.make_async_copy(out.at[:, pl.ds(0, 2048)], out.at[:, pl.ds(0, 2048)], out_own).wait()
    pltpu.make_async_copy(out.at[:, pl.ds(0, 6144)], out.at[:, pl.ds(0, 6144)], out_send).wait()
    pltpu.make_async_copy(out.at[:, pl.ds(0, 6144)], out.at[:, pl.ds(0, 6144)], out_recv).wait()


def fused(number, src, post, where, counts, over, queries, k_own, v_own, k_twin):
    vmem = lambda *shape: pltpu.VMEM((*shape, BLK, HD), jnp.bfloat16)
    smem, whole = pl.BlockSpec(memory_space=pltpu.SMEM), pl.BlockSpec(memory_space=pltpu.VMEM)
    anywhere = pl.BlockSpec(memory_space=pl.ANY)
    dma = pltpu.SemaphoreType.DMA
    return pl.pallas_call(
        fused_kernel,
        out_shape=(jax.ShapeDtypeStruct((96, 8192), jnp.bfloat16), jax.ShapeDtypeStruct((1, 128), jnp.int32)),
        in_specs=[smem, smem, smem, smem, whole, *[anywhere] * 4],
        out_specs=(anywhere, whole),
        scratch_shapes=[
            vmem(256), vmem(256), vmem(2 * USUAL[0]), vmem(NZ * NW * 6),
            *[vmem(2 * c) for c in USUAL] * 2,
            vmem(NZ * NW * 6), vmem(NZ * NW * 6), vmem(5 * 64),
            pltpu.VMEM((384, 16, HD), jnp.bfloat16),
            pltpu.VMEM((384, 2048), jnp.bfloat16),
            pltpu.VMEM((BLK * 16, HD), jnp.float32),
            pltpu.VMEM((SEL * BLK, HD), jnp.bfloat16),
            pltpu.VMEM((SEL * BLK, 2 * HD), jnp.bfloat16),
            pltpu.VMEM((NW, 1, 128), jnp.int32),
            pltpu.VMEM((4, 1, 128), jnp.int32),
            dma, dma((2, 2)), dma, dma((2, 2, 10)), dma((2, 2, 10)), dma((2, NZ)), dma((2,)), dma((2, NZ)),
            dma((NW + 4,)), dma((NW + 4,)), dma, dma, dma,
        ],
        compiler_params=pltpu.CompilerParams(
            collective_id=number, has_side_effects=True, vmem_limit_bytes=60 * 2**20
        ),
        name="fused",
    )(src, post, where, counts, over, queries, k_own, v_own, k_twin)


def own_requests(blocks, counts):
    me = lax.axis_index("ctx")
    z = me // NW
    flat = blocks.reshape(-1)
    ids = np.arange(ITEMS * SEL)
    live = (jnp.asarray(ids % SEL)[None, :].reshape(ITEMS, SEL) < counts.reshape(ITEMS, 1)).reshape(-1)
    holder = jnp.where(live, flat // BLK, -1)
    earlier = jnp.asarray(ids[None, :] < ids[:, None])
    rank = jnp.sum(((holder[:, None] == holder[None, :]) & earlier).astype(jnp.int32), axis=1)
    core = holder % 2
    lane = (holder // 2 % 4) * 2 + (rank + core) % 2
    away = (z - holder // NW + NZ) % NZ
    inside = core * 3 + rank // 2
    tile = core * 128 + jnp.asarray(ids // SEL % 2) * BLK + flat % BLK + 1
    slot = jnp.where(live, lane * 48 + away * 6 + inside, -1)
    mine = jnp.sum(jnp.where(slot[None, :] == jnp.arange(NW * 48)[:, None], tile[None, :], 0), axis=1)
    mine = jnp.pad(mine.reshape(NW, 1, 48), ((0, 0), (0, 0), (0, 80)))
    where = jnp.where(live, away * 48 + lane * 6 + inside, 0)
    return mine, where


def full_plan(table):
    asked = table[:, :, :48].reshape(NZ, NW, NZ, 6)
    by_k = [jnp.roll(asked[:, :, k], -k, axis=0) for k in range(NZ)]
    up = [by_k[4][:, 0::2], by_k[3], by_k[2], by_k[1]]
    down = [by_k[4][:, 1::2], by_k[5], by_k[6], by_k[7]]
    lists = jnp.stack([jnp.concatenate([e.reshape(NZ, -1) for e in way], axis=1) for way in (up, down)])
    live = lists > 0
    size = lists.shape[2]
    before = jnp.asarray(np.triu(np.ones((size, size), np.float32), 1))
    at = jnp.dot(live.reshape(-1, size).astype(jnp.float32), before).astype(jnp.int32).reshape(lists.shape)
    hit = (at[:, 0, None, :] == jnp.arange(size)[None, :, None]) & live[:, 0, None, :]
    src = jnp.maximum(jnp.sum(jnp.where(hit, lists[:, 0, None, :], 0), axis=2) - 1, 0)

    def seg(d, k, part):
        lo, hi = (0, 24) if part == 0 else (24 + 48 * (part - 1), 24 + 48 * part)
        return jnp.minimum(at[d, (NZ - k) % NZ, lo:hi], FULL[3 - part] - 1) + d * FULL[3 - part]

    here = jnp.maximum(by_k[0][0] - 1, 0)
    four = jnp.stack([seg(0, 4, 0).reshape(4, 6), seg(1, 4, 0).reshape(4, 6)], axis=1)
    parts = [here, seg(0, 1, 3), seg(0, 2, 2), seg(0, 3, 1), four, seg(1, 5, 1), seg(1, 6, 2), seg(1, 7, 3)]
    return src, jnp.concatenate([p.reshape(NW, 6) for p in parts], axis=1)


def per_device(queries, keys, values, sel_blocks, sel_counts):
    k_own = keys.reshape(128, BLK, HD)
    v_own = values.reshape(128, BLK, HD)
    mine, where = own_requests(sel_blocks, sel_counts)
    counts = sel_counts.reshape(-1)
    table, src, post, over, k_twin = exchange_requests(mine, k_own)
    out, over = fused(1, src, post, where, counts, over, queries, k_own, v_own, k_twin)

    def again():
        src, post = full_plan(table)
        none = jnp.zeros((1, 128), jnp.int32)
        k, _ = exchange_tiles(2, FULL, src, post, none, (k_own,), (None,))
        v, _ = exchange_tiles(3, FULL, src, post, none, (v_own,), (None,))
        return attend_all(4, where, counts, none, queries, k, v)[0]

    return lax.cond(over[0, 0] > 0, again, lambda: out)


def solution(mesh):
    placed = (
        P("ctx", "head", None),
        P("head", "ctx", None),
        P("head", "ctx", None),
        P("ctx", "head", None),
        P("ctx", "head"),
    )
    return jax.shard_map(
        per_device, mesh=mesh, in_specs=placed, out_specs=P(("ctx", "head"), None), check_vma=False
    )
```

```python
import jax
import jax.numpy as jnp
import numpy as np
from jax import lax
from jax.experimental import pallas as pl
from jax.experimental.pallas import tpu as pltpu
from jax.sharding import PartitionSpec as P

BLK = 64
HD = 128
SEL = 16
ITEMS = 12
NZ = 8
NW = 8
STEPS = 4
USUAL = (104, 78, 50, 24)
FULL = (168, 120, 72, 24)
MESH = pl.DeviceIdType.MESH


def at_ctx(index):
    return {"ctx": index}


def tiles_kernel(caps, arrays, fetch, src, post, over, *refs):
    cuts = (0, *caps[::-1])
    refs = list(refs)
    take = lambda n: [refs.pop(0) for _ in range(n)]
    owns = take(arrays)
    twins = [None if f else refs.pop(0) for f in fetch]
    outs, over_out = take(arrays), refs.pop(0)
    tab, lists, stage = take(arrays), take(arrays), take(arrays)
    hops = [take(STEPS) for _ in range(arrays)]
    overs, tab_sem, twin_send, z_send, z_recv, y_send, y_recv, y_local, over_send, over_recv = refs
    me = lax.axis_index("ctx")
    z, w = me // NW, me % NW
    core = me % 2
    twin_at = me + 1 - 2 * core
    towards = (((z + 1) % NZ) * NW + w, ((z + NZ - 1) % NZ) * NW + w)

    barrier = pltpu.get_barrier_semaphore()
    for other in towards:
        pl.semaphore_signal(barrier, inc=1, device_id=at_ctx(other), device_id_type=MESH)
    for r in range(1, NW):
        pl.semaphore_signal(barrier, inc=1, device_id=at_ctx(z * NW + (w + r) % NW), device_id_type=MESH)
    pl.semaphore_wait(barrier, NW + 1)

    loads = []
    for a in range(arrays):
        mine = tab[a].at[pl.ds(core * 128, 128)]
        pair = [pltpu.make_async_copy(owns[a], mine, tab_sem.at[a, 0])]
        if fetch[a]:
            pair.append(
                pltpu.make_async_remote_copy(
                    src_ref=owns[a], dst_ref=mine, send_sem=twin_send.at[a], recv_sem=tab_sem.at[a, 1],
                    device_id=at_ctx(twin_at), device_id_type=MESH,
                )
            )
        else:
            pair.append(
                pltpu.make_async_copy(twins[a], tab[a].at[pl.ds((1 - core) * 128, 128)], tab_sem.at[a, 1])
            )
        for copy in pair:
            copy.start()
        loads.append(pair)
    told = []
    for r in range(1, NW):
        copy = pltpu.make_async_remote_copy(
            src_ref=over, dst_ref=overs.at[r], send_sem=over_send.at[r], recv_sem=over_recv.at[r],
            device_id=at_ctx(z * NW + (w + r) % NW), device_id_type=MESH,
        )
        copy.start()
        told.append(copy)

    def hop(a, d, step, piece):
        lo, hi = cuts[piece], cuts[piece + 1]
        source = lists[a] if step == 1 else hops[a][step - 2]
        number = (0, 4, 7, 9)[step - 1] + piece
        return pltpu.make_async_remote_copy(
            src_ref=source.at[pl.ds(d * caps[max(step - 2, 0)] + lo, hi - lo)],
            dst_ref=hops[a][step - 1].at[pl.ds(d * caps[step - 1] + lo, hi - lo)],
            send_sem=z_send.at[a, d, number],
            recv_sem=z_recv.at[a, d, number],
            device_id=at_ctx(towards[d]),
            device_id_type=MESH,
        )

    def pack(a, piece):
        for d in range(2):
            def one(i, carry):
                lists[a][d * caps[0] + i] = tab[a][src[d, i]]
                return carry

            lax.fori_loop(cuts[piece], cuts[piece + 1], one, 0)

    def deliver(a, k):
        base = k * NW * 6
        source = tab[a] if k == 0 else hops[a][min(k, NZ - k) - 1]

        def one(i, carry):
            for j in range(6):
                stage[a][base + i * 6 + j] = source[post[i, k * 6 + j]]
            return carry

        lax.fori_loop(0, NW, one, 0)

        def send(r, carry):
            ow = (w + r) % NW
            pltpu.make_async_remote_copy(
                src_ref=stage[a].at[pl.ds(base + ow * 6, 6)],
                dst_ref=outs[a].at[pl.ds(base + w * 6, 6)],
                send_sem=y_send.at[a],
                recv_sem=y_recv.at[a],
                device_id=at_ctx(z * NW + ow),
                device_id_type=MESH,
            ).start()
            return carry

        lax.fori_loop(1, NW, send, 0)
        pltpu.make_async_copy(
            stage[a].at[pl.ds(base + w * 6, 6)], outs[a].at[pl.ds(base + w * 6, 6)], y_local.at[a]
        ).start()

    def arrive_and_pass(a, step):
        for piece in range(5 - step):
            for d in range(2):
                hop(a, d, step, piece).wait_recv()
                if piece < 4 - step:
                    hop(a, d, step + 1, piece).start()

    def start_first(a):
        for piece in range(STEPS):
            for d in range(2):
                hop(a, d, 1, piece).start()

    for copy in loads[0]:
        copy.wait()
    for piece in range(STEPS):
        pack(0, piece)
        for d in range(2):
            hop(0, d, 1, piece).start()
    if arrays == 2:
        for copy in loads[1]:
            copy.wait()
        for piece in range(STEPS):
            pack(1, piece)
    deliver(0, 0)
    arrive_and_pass(0, 1)
    if arrays == 2:
        start_first(1)
        deliver(1, 0)
    for a in range(arrays):
        if a:
            arrive_and_pass(a, 1)
        for step in range(1, STEPS):
            deliver(a, step)
            deliver(a, NZ - step)
            arrive_and_pass(a, step + 1)
        deliver(a, STEPS)
    for a in range(arrays):
        for d in range(2):
            for step in range(1, STEPS + 1):
                for piece in range(STEPS + 1 - step):
                    hop(a, d, step, piece).wait_send()
    most = over[...]
    for r, copy in enumerate(told):
        copy.wait()
        most = jnp.maximum(most, overs[r + 1])
    over_out[...] = most
    remote, local = NZ * (NW - 1) * 6, NZ * 6
    for a in range(arrays):
        pltpu.make_async_copy(stage[a].at[pl.ds(0, remote)], stage[a].at[pl.ds(0, remote)], y_send.at[a]).wait()
        pltpu.make_async_copy(outs[a].at[pl.ds(0, remote)], outs[a].at[pl.ds(0, remote)], y_recv.at[a]).wait()
        pltpu.make_async_copy(outs[a].at[pl.ds(0, local)], outs[a].at[pl.ds(0, local)], y_local.at[a]).wait()


def exchange_tiles(number, caps, src, post, over, owns, twins):
    n = len(owns)
    fetch = tuple(t is None for t in twins)
    given = [t for t in twins if t is not None]
    tiles = jax.ShapeDtypeStruct((NZ * NW * 6, BLK, HD), owns[0].dtype)
    vmem = lambda *shape: pltpu.VMEM((*shape, BLK, HD), jnp.bfloat16)
    smem, whole = pl.BlockSpec(memory_space=pltpu.SMEM), pl.BlockSpec(memory_space=pltpu.VMEM)
    anywhere = pl.BlockSpec(memory_space=pl.ANY)
    dma = pltpu.SemaphoreType.DMA
    return pl.pallas_call(
        lambda *refs: tiles_kernel(caps, n, fetch, *refs),
        out_shape=(*[tiles] * n, jax.ShapeDtypeStruct((1, 128), jnp.int32)),
        in_specs=[smem, smem, whole, *[anywhere] * (n + len(given))],
        out_specs=(*[anywhere] * n, whole),
        scratch_shapes=[
            *[vmem(256)] * n,
            *[vmem(2 * caps[0])] * n,
            *[vmem(NZ * NW * 6)] * n,
            *[vmem(2 * c) for c in caps] * n,
            pltpu.VMEM((NW, 1, 128), jnp.int32),
            dma((n, 2)), dma((n,)), dma((n, 2, 10)), dma((n, 2, 10)),
            dma((n,)), dma((n,)), dma((n,)), dma((NW,)), dma((NW,)),
        ],
        compiler_params=pltpu.CompilerParams(
            collective_id=number, has_side_effects=True, vmem_limit_bytes=60 * 2**20
        ),
        name="tiles",
    )(src, post, over, *owns, *given)


def attend_kernel(where, counts, over, q, k, v, out, over_out, merged, qf, kc, vc, overs, send_sem, recv_sem, own_sem, over_send, over_recv):
    me = lax.axis_index("head")
    barrier = pltpu.get_barrier_semaphore()
    for r in range(1, 4):
        pl.semaphore_signal(barrier, inc=1, device_id={"head": (me + r) % 4}, device_id_type=MESH)
    pl.semaphore_wait(barrier, 3)
    told = []
    for r in range(1, 4):
        copy = pltpu.make_async_remote_copy(
            src_ref=over, dst_ref=overs.at[r], send_sem=over_send.at[r], recv_sem=over_recv.at[r],
            device_id={"head": (me + r) % 4}, device_id_type=MESH,
        )
        copy.start()
        told.append(copy)
    keys = SEL * BLK
    factor = float(HD ** -0.5 * np.log2(np.e))
    vc[:, HD:] = jnp.ones((keys, HD), jnp.bfloat16)
    first = ((me + 1) * 3 // 2) % 6

    def one_block(i, carry):
        b = (first + i) % 6
        qf[...] = q[pl.ds(b * BLK, BLK)].astype(jnp.float32).reshape(BLK * 16, HD)
        for g in range(2):
            item = b * 2 + g

            def gather(s, c):
                at = where[item * SEL + s]
                kc[pl.ds(s * BLK, BLK)] = k[at]
                vc[pl.ds(s * BLK, BLK), 0:HD] = v[at]
                return c

            lax.fori_loop(0, SEL, gather, 0)
            rows = jnp.concatenate(
                [qf[pl.ds(g * 8 + h, BLK, stride=16)].astype(jnp.bfloat16) for h in range(8)], axis=0
            )
            s = lax.dot_general(rows, kc[...], (((1,), (1,)), ((), ())), preferred_element_type=jnp.float32)
            kept = lax.broadcasted_iota(jnp.int32, (1, keys), 1) < counts[item] * BLK
            s = jnp.where(kept, s, -jnp.inf)
            top = jnp.max(s, axis=1, keepdims=True)
            p = jnp.exp2((s - top) * factor).astype(jnp.bfloat16)
            o = jnp.dot(p, vc[...], preferred_element_type=jnp.float32)
            o = o[:, 0:HD] / o[:, HD:]
            for h in range(8):
                merged[pl.ds(b * BLK, BLK), pl.ds(g * 1024 + h * HD, HD)] = o[h * BLK:(h + 1) * BLK].astype(jnp.bfloat16)
        for half in range(2):
            unit = b * 2 + half
            to = unit // 3
            source = merged.at[pl.ds(unit * 32, 32)]
            target = out.at[pl.ds((unit % 3) * 32, 32), pl.ds(pl.multiple_of(me * 2048, 2048), 2048)]

            @pl.when(to == me)
            def _():
                pltpu.make_async_copy(source, target, own_sem).start()

            @pl.when(to != me)
            def _():
                pltpu.make_async_remote_copy(
                    src_ref=source, dst_ref=target, send_sem=send_sem, recv_sem=recv_sem,
                    device_id={"head": to}, device_id_type=MESH,
                ).start()
        return carry

    lax.fori_loop(0, 6, one_block, 0)
    most = over[...]
    for r, copy in enumerate(told):
        copy.wait()
        most = jnp.maximum(most, overs[r + 1])
    over_out[...] = most
    pltpu.make_async_copy(out.at[:, pl.ds(0, 2048)], out.at[:, pl.ds(0, 2048)], own_sem).wait()
    pltpu.make_async_copy(out.at[:, pl.ds(0, 6144)], out.at[:, pl.ds(0, 6144)], send_sem).wait()
    pltpu.make_async_copy(out.at[:, pl.ds(0, 6144)], out.at[:, pl.ds(0, 6144)], recv_sem).wait()


def attend_all(number, where, counts, over, queries, k, v):
    smem, vmem = pl.BlockSpec(memory_space=pltpu.SMEM), pl.BlockSpec(memory_space=pltpu.VMEM)
    dma = pltpu.SemaphoreType.DMA
    return pl.pallas_call(
        attend_kernel,
        out_shape=(jax.ShapeDtypeStruct((96, 8192), jnp.bfloat16), jax.ShapeDtypeStruct((1, 128), jnp.int32)),
        in_specs=[smem, smem, vmem, vmem, vmem, vmem],
        out_specs=(pl.BlockSpec(memory_space=pl.ANY), vmem),
        scratch_shapes=[
            pltpu.VMEM((384, 2048), jnp.bfloat16),
            pltpu.VMEM((BLK * 16, HD), jnp.float32),
            pltpu.VMEM((SEL * BLK, HD), jnp.bfloat16),
            pltpu.VMEM((SEL * BLK, 2 * HD), jnp.bfloat16),
            pltpu.VMEM((4, 1, 128), jnp.int32),
            dma, dma, dma, dma((4,)), dma((4,)),
        ],
        compiler_params=pltpu.CompilerParams(
            collective_id=number, has_side_effects=True, vmem_limit_bytes=60 * 2**20
        ),
        name="attend",
    )(where, counts, over, queries, k, v)


def fused_kernel(
    asks, within, same, lower, column, counts, q_in, k_own, v_own, out, over_out, table, where_v,
    tab_k, tab_v, packed, stage, k1, k2, k3, k4, v1, v2, v3, v4, land_k, land_v, more,
    q, merged, qf, kc, vc, overs, overs_head, mine, rows, src_v, post_v, src, post, where,
    q_sem, tab_sem, twin_send, z_send, z_recv, y_send, y_recv, y_local,
    over_send, over_recv, out_send, out_recv, out_own, local_sem, ask_send, ask_recv, plan_sem,
):
    caps = USUAL
    cuts = (0, *caps[::-1])
    tab, land, hops = (tab_k, tab_v), (land_k, land_v), ((k1, k2, k3, k4), (v1, v2, v3, v4))
    me = lax.axis_index("ctx")
    head = lax.axis_index("head")
    z, w = me // NW, me % NW
    core = me % 2
    towards = (((z + 1) % NZ) * NW + w, ((z + NZ - 1) % NZ) * NW + w)

    barrier = pltpu.get_barrier_semaphore()
    for r in range(1, 8):
        pl.semaphore_signal(barrier, inc=1, device_id=at_ctx(z * NW + (w + r) % NW), device_id_type=MESH)
        pl.semaphore_signal(barrier, inc=1, device_id=at_ctx((z + r) % NZ * NW + w), device_id_type=MESH)
    for r in range(1, 4):
        pl.semaphore_signal(barrier, inc=1, device_id={"head": (head + r) % 4}, device_id_type=MESH)

    size = asks.shape[1]
    ask = asks[...]
    across = jnp.broadcast_to(ask.astype(jnp.float32), (size, size))
    down = across.T.astype(jnp.int32)
    i0 = lax.broadcasted_iota(jnp.int32, (size, size), 0)
    i1 = lax.broadcasted_iota(jnp.int32, (size, size), 1)
    earlier = ((down >> 6) == (jnp.broadcast_to(ask, (size, size)) >> 6)) & (i0 < i1)
    rank = jnp.sum(earlier.astype(jnp.float32), axis=0, keepdims=True).astype(jnp.int32)
    used = ask >= 0
    holder = ask >> 6
    its_core = holder & 1
    lane = ((holder >> 1) & 3) * 2 + ((rank + its_core) & 1)
    away = (z - (holder >> 3) + NZ) & 7
    inside = its_core * 3 + (rank >> 1)
    group = (lax.broadcasted_iota(jnp.int32, (1, size), 1) >> 4) & 1
    tile = its_core * 128 + group * BLK + (ask & 63) + 1
    where_v[...] = jnp.clip(jnp.where(used, away * 48 + lane * 6 + inside, 0), 0, NZ * NW * 6 - 1)
    to_lane = lax.broadcasted_iota(jnp.int32, (NW, size), 0) == jnp.where(used, lane, -1)
    to_slot = lax.broadcasted_iota(jnp.int32, (128, size), 0) == away * 6 + inside
    asked_of = lax.dot_general(
        jnp.where(to_lane, tile.astype(jnp.float32), 0.0), to_slot.astype(jnp.float32),
        (((1,), (1,)), ((), ())), preferred_element_type=jnp.float32,
    ).astype(jnp.int32)
    for i in range(NW):
        mine[i] = asked_of[i:i + 1]

    pl.semaphore_wait(barrier, 17)

    asking = []
    for r in range(1, NW):
        ow = (w + r) % NW
        copy = pltpu.make_async_remote_copy(
            src_ref=mine.at[pl.ds(ow, 1)], dst_ref=rows.at[pl.ds(w, 1)],
            send_sem=ask_send.at[r], recv_sem=ask_recv.at[r],
            device_id=at_ctx(z * NW + ow), device_id_type=MESH,
        )
        copy.start()
        asking.append(copy)
    own = pltpu.make_async_copy(mine.at[pl.ds(w, 1)], rows.at[pl.ds(w, 1)], local_sem)
    own.start()

    mine_k, mine_v = (t.at[pl.ds(core * 128, 128)] for t in tab)
    loads = []
    for a, (ref, near) in enumerate(((k_own, mine_k), (v_own, mine_v))):
        pair = (
            pltpu.make_async_copy(ref, near, tab_sem.at[a, 0]),
            pltpu.make_async_remote_copy(
                src_ref=ref, dst_ref=near, send_sem=twin_send.at[a], recv_sem=tab_sem.at[a, 1],
                device_id=at_ctx(me + 1 - 2 * core), device_id_type=MESH,
            ),
        )
        for copy in pair:
            copy.start()
        loads.append(pair)
    q_load = pltpu.make_async_copy(q_in, q, q_sem)
    q_load.start()

    own.wait()
    for copy in asking:
        copy.wait()
    table[0] = jnp.concatenate([rows[i] for i in range(NW)], axis=0)
    asking = []
    for r in range(1, NZ):
        copy = pltpu.make_async_remote_copy(
            src_ref=table.at[0], dst_ref=table.at[NZ - r],
            send_sem=ask_send.at[NW + r], recv_sem=ask_recv.at[NW + r],
            device_id=at_ctx((z + r) % NZ * NW + w), device_id_type=MESH,
        )
        copy.start()
        asking.append(copy)
    for copy in asking:
        copy.wait()

    kind = (lax.broadcasted_iota(jnp.int32, (NW, 128), 1) * 43) >> 8
    asked = [table[i] for i in range(NZ)]
    by_source = []
    for i in range(NZ):
        row = jnp.zeros((NW, 128), jnp.int32)
        for k in range(NZ):
            row = jnp.where(kind == k, asked[(i + k) % NZ], row)
        by_source.append(row)
    tiles = jnp.concatenate(by_source, axis=0)
    kind = jnp.concatenate([kind] * NZ, axis=0)
    live = tiles > 0
    ones = live.astype(jnp.float32)
    dot = lambda x, y: jnp.dot(x, y, preferred_element_type=jnp.float32)
    per_row = dot(ones, same[...])
    at = dot(ones, within[...]) + dot(lower[...], per_row)
    sums = dot(column[...], per_row)
    n = [sums[:, 6 * k:6 * k + 1] for k in range(NZ)]
    c1, c2, c3, c4 = (float(c) for c in USUAL)
    least = lambda x, y, t: jnp.minimum(
        jnp.minimum(jnp.full_like(x, c4), c3 - x), jnp.minimum(c2 - x - y, c1 - x - y - t)
    )
    room_up, room_down = least(n[3], n[2], n[1]), least(n[5], n[6], n[7])
    four_up = jnp.clip(room_up, 0.0, n[4])
    four_down = n[4] - four_up
    short = (room_up < 0) | (room_down < 0) | (four_down > room_down)
    over = jnp.broadcast_to(jnp.max(short.astype(jnp.float32), axis=0, keepdims=True), (1, 128)).astype(jnp.int32)
    up = (kind < 4) | ((kind == 4) & (at < four_up))
    base = jnp.zeros_like(at)
    for k, first in (
        (3, four_up), (2, four_up + n[3]), (1, four_up + n[3] + n[2]),
        (5, four_down), (6, four_down + n[5]), (7, four_down + n[5] + n[6]),
    ):
        base = jnp.where(kind == k, first, base)
    base = jnp.where((kind == 4) & (at >= four_up), -four_up, base)
    at = at + base

    places = lax.broadcasted_iota(jnp.int32, (128, 128), 0).astype(jnp.float32)
    found = []
    for way in range(2):
        mine_too = live[0:NW] & (up[0:NW] if way == 0 else ~up[0:NW]) & (kind[0:NW] > 0)
        place = jnp.where(mine_too, at[0:NW], -1.0)
        value = jnp.where(mine_too, tiles[0:NW], 0).astype(jnp.float32)
        total = jnp.zeros((128, 128), jnp.float32)
        for i in range(NW):
            total = jnp.where(place[i:i + 1] == places, value[i:i + 1], total)
        found.append(
            lax.dot_general(
                jnp.ones((8, 128), jnp.float32), total, (((1,), (1,)), ((), ())), preferred_element_type=jnp.float32
            )
        )
    row = lax.broadcasted_iota(jnp.int32, (8, 128), 0)
    src_v[...] = jnp.clip(jnp.where(row == 0, found[0], found[1]).astype(jnp.int32) - 1, 0, 255)

    cap = jnp.full((NZ * NW, 128), USUAL[0], jnp.int32)
    for k in range(2, 7):
        cap = jnp.where(kind == k, USUAL[min(k, NZ - k) - 1], cap)
    spot = jnp.clip(at.astype(jnp.int32), 0, cap - 1) + jnp.where(up, 0, cap)
    mine_at = jnp.clip(tiles[0:NW] - 1, 0, 255)
    for k in range(1, NZ):
        i = NZ - k
        mine_at = jnp.where(kind[0:NW] == k, spot[i * NW:(i + 1) * NW], mine_at)
    post_v[...] = mine_at
    moves = [
        pltpu.make_async_copy(ref, to, plan_sem.at[i])
        for i, (ref, to) in enumerate(((src_v, src), (post_v, post), (where_v, where)))
    ]
    for copy in moves:
        copy.start()
    for copy in moves:
        copy.wait()
    overs[0] = over
    told = []
    for r in range(1, NW):
        copy = pltpu.make_async_remote_copy(
            src_ref=overs.at[0], dst_ref=overs.at[r], send_sem=over_send.at[r], recv_sem=over_recv.at[r],
            device_id=at_ctx(z * NW + (w + r) % NW), device_id_type=MESH,
        )
        copy.start()
        told.append(copy)

    def hop(a, d, step, piece):
        lo, hi = cuts[piece], cuts[piece + 1]
        source = packed if step == 1 else hops[a][step - 2]
        number = (0, 4, 7, 9)[step - 1] + piece
        return pltpu.make_async_remote_copy(
            src_ref=source.at[pl.ds(d * caps[max(step - 2, 0)] + lo, hi - lo)],
            dst_ref=hops[a][step - 1].at[pl.ds(d * caps[step - 1] + lo, hi - lo)],
            send_sem=z_send.at[a, d, number],
            recv_sem=z_recv.at[a, d, number],
            device_id=at_ctx(towards[d]),
            device_id_type=MESH,
        )

    def pack_and_start(a):
        for piece in range(STEPS):
            for d in range(2):
                def one(i, carry):
                    packed[d * caps[0] + i] = tab[a][src[d, i]]
                    return carry

                lax.fori_loop(cuts[piece], cuts[piece + 1], one, 0)
                hop(a, d, 1, piece).start()

    def settle(a, k):
        pltpu.make_async_copy(stage.at[pl.ds(0, 42)], stage.at[pl.ds(0, 42)], y_send.at[a, k]).wait()
        pltpu.make_async_copy(stage.at[pl.ds(0, 6)], stage.at[pl.ds(0, 6)], y_local.at[a, k]).wait()

    def deliver(a, k):
        base = k * NW * 6
        source = tab[a] if k == 0 else hops[a][min(k, NZ - k) - 1]
        if a and k != STEPS:
            settle(0, k)

        def one(i, carry):
            for j in range(6):
                stage[base + i * 6 + j] = source[post[i, k * 6 + j]]
            return carry

        lax.fori_loop(0, NW, one, 0)

        def send(r, carry):
            ow = (w + r) % NW
            pltpu.make_async_remote_copy(
                src_ref=stage.at[pl.ds(base + ow * 6, 6)],
                dst_ref=land[a].at[pl.ds(base + w * 6, 6)],
                send_sem=y_send.at[a, k],
                recv_sem=y_recv.at[a],
                device_id=at_ctx(z * NW + ow),
                device_id_type=MESH,
            ).start()
            return carry

        lax.fori_loop(1, NW, send, 0)
        pltpu.make_async_copy(
            stage.at[pl.ds(base + w * 6, 6)], land[a].at[pl.ds(base + w * 6, 6)], y_local.at[a, k]
        ).start()

    def arrive_and_pass(a, step):
        for piece in range(5 - step):
            for d in range(2):
                hop(a, d, step, piece).wait_recv()
                if piece < 4 - step:
                    hop(a, d, step + 1, piece).start()

    def all_landed(a):
        remote = NZ * (NW - 1) * 6
        pltpu.make_async_copy(land[a].at[pl.ds(0, remote)], land[a].at[pl.ds(0, remote)], y_recv.at[a]).wait()

    keys = SEL * BLK
    factor = float(HD ** -0.5 * np.log2(np.e))
    first = ((head + 1) * 3 // 2) % 6 * 2

    def weigh(ref, n, spot):
        item = (first + n) % ITEMS
        b, g = item // 2, item % 2
        qf[...] = q[pl.ds(b * BLK, BLK)].astype(jnp.float32).reshape(BLK * 16, HD)

        def gather(i, c):
            kc[pl.ds(i * BLK, BLK)] = land_k[where[0, item * SEL + i]]
            return c

        lax.fori_loop(0, SEL, gather, 0)
        rows = jnp.concatenate(
            [qf[pl.ds(g * 8 + h, BLK, stride=16)].astype(jnp.bfloat16) for h in range(8)], axis=0
        )
        s = lax.dot_general(rows, kc[...], (((1,), (1,)), ((), ())), preferred_element_type=jnp.float32)
        kept = lax.broadcasted_iota(jnp.int32, (1, keys), 1) < counts[item] * BLK
        s = jnp.where(kept, s, -jnp.inf)
        top = jnp.max(s, axis=1, keepdims=True)
        p = jnp.exp2((s - top) * factor).astype(jnp.bfloat16)
        for h in range(8):
            for c in range(8):
                ref[spot * 64 + h * 8 + c] = p[h * BLK:(h + 1) * BLK, c * HD:(c + 1) * HD]

    def finish(ref, n, spot):
        item = (first + n) % ITEMS
        b, g = item // 2, item % 2

        def gather(i, c):
            vc[pl.ds(i * BLK, BLK), 0:HD] = land_v[where[0, item * SEL + i]]
            return c

        lax.fori_loop(0, SEL, gather, 0)
        p = jnp.concatenate(
            [jnp.concatenate([ref[spot * 64 + h * 8 + c] for c in range(8)], axis=1) for h in range(8)], axis=0
        )
        o = jnp.dot(p, vc[...], preferred_element_type=jnp.float32)
        o = (o[:, 0:HD] / o[:, HD:]).astype(jnp.bfloat16)
        for h in range(8):
            merged[pl.ds(b * BLK, BLK), pl.ds(pl.multiple_of(g * 1024 + h * HD, HD), HD)] = o[h * BLK:(h + 1) * BLK]

        @pl.when(g == 1)
        def _():
            for half in range(2):
                unit = b * 2 + half
                to = unit // 3
                source = merged.at[pl.ds(unit * 32, 32)]
                target = out.at[pl.ds((unit % 3) * 32, 32), pl.ds(pl.multiple_of(head * 2048, 2048), 2048)]

                @pl.when(to == head)
                def _():
                    pltpu.make_async_copy(source, target, out_own).start()

                @pl.when(to != head)
                def _():
                    pltpu.make_async_remote_copy(
                        src_ref=source, dst_ref=target, send_sem=out_send, recv_sem=out_recv,
                        device_id={"head": to}, device_id_type=MESH,
                    ).start()

    def over_items(work, ref, lo, hi):
        def one(n, carry):
            work(ref, n, n - lo)
            return carry

        lax.fori_loop(lo, hi, one, 0)

    for copy in loads[0]:
        copy.wait()
    pack_and_start(0)
    deliver(0, 0)
    arrive_and_pass(0, 1)
    for piece in range(STEPS):
        for d in range(2):
            hop(0, d, 1, piece).wait_send()
    for copy in loads[1]:
        copy.wait()
    pack_and_start(1)
    deliver(1, 0)
    deliver(0, 1)
    deliver(0, 7)
    arrive_and_pass(0, 2)
    deliver(0, 2)
    deliver(0, 6)
    arrive_and_pass(1, 1)
    deliver(1, 1)
    deliver(1, 7)
    arrive_and_pass(0, 3)
    deliver(0, 3)
    deliver(0, 5)
    arrive_and_pass(1, 2)
    deliver(1, 2)
    deliver(1, 6)
    arrive_and_pass(0, 4)
    deliver(0, 4)
    for step in range(2, STEPS + 1):
        for piece in range(STEPS + 1 - step):
            for d in range(2):
                hop(0, d, step, piece).wait_send()
    arrive_and_pass(1, 3)
    deliver(1, 3)
    deliver(1, 5)
    vc[:, HD:] = jnp.ones((keys, HD), jnp.bfloat16)
    q_load.wait()
    most = over
    for r, copy in enumerate(told):
        copy.wait()
        most = jnp.maximum(most, overs[r + 1])
    overs_head[0] = most
    told = []
    for r in range(1, 4):
        copy = pltpu.make_async_remote_copy(
            src_ref=overs_head.at[0], dst_ref=overs_head.at[r], send_sem=over_send.at[NW + r], recv_sem=over_recv.at[NW + r],
            device_id={"head": (head + r) % 4}, device_id_type=MESH,
        )
        copy.start()
        told.append(copy)
    settle(0, STEPS)
    all_landed(0)
    over_items(weigh, tab_k, 0, 4)
    arrive_and_pass(1, 4)
    deliver(1, 4)
    over_items(weigh, k1, 4, 7)
    over_items(weigh, more, 7, ITEMS)
    for step in range(1, STEPS + 1):
        for piece in range(STEPS + 1 - step):
            for d in range(2):
                hop(1, d, step, piece).wait_send()
    for k in range(NZ):
        settle(1, k)
    all_landed(1)
    over_items(finish, tab_k, 0, 4)
    over_items(finish, k1, 4, 7)
    over_items(finish, more, 7, ITEMS)
    for r, copy in enumerate(told):
        copy.wait()
        most = jnp.maximum(most, overs_head[r + 1])
    over_out[...] = most
    pltpu.make_async_copy(out.at[:, pl.ds(0, 2048)], out.at[:, pl.ds(0, 2048)], out_own).wait()
    pltpu.make_async_copy(out.at[:, pl.ds(0, 6144)], out.at[:, pl.ds(0, 6144)], out_send).wait()
    pltpu.make_async_copy(out.at[:, pl.ds(0, 6144)], out.at[:, pl.ds(0, 6144)], out_recv).wait()


def fused(number, asks, counts, queries, k_own, v_own):
    vmem = lambda *shape: pltpu.VMEM((*shape, BLK, HD), jnp.bfloat16)
    ints = lambda *shape: pltpu.VMEM(shape, jnp.int32)
    smem, whole = pl.BlockSpec(memory_space=pltpu.SMEM), pl.BlockSpec(memory_space=pltpu.VMEM)
    anywhere = pl.BlockSpec(memory_space=pl.ANY)
    dma = pltpu.SemaphoreType.DMA
    lane, row = np.arange(128), np.arange(NZ * NW)
    block = (lane[:, None] // 6 == lane[None, :] // 6) & (lane[:, None] < 48)
    plane = row[:, None] // NW == row[None, :] // NW
    within = (block & (lane[:, None] < lane[None, :])).astype(np.float32)
    lower = (plane & (row[None, :] < row[:, None])).astype(np.float32)
    return pl.pallas_call(
        fused_kernel,
        out_shape=(
            jax.ShapeDtypeStruct((96, 8192), jnp.bfloat16),
            jax.ShapeDtypeStruct((1, 128), jnp.int32),
            jax.ShapeDtypeStruct((NZ, NW, 128), jnp.int32),
            jax.ShapeDtypeStruct(asks.shape, jnp.int32),
        ),
        in_specs=[*[whole] * 5, smem, *[anywhere] * 3],
        out_specs=(anywhere, whole, whole, whole),
        scratch_shapes=[
            vmem(256), vmem(256), vmem(2 * USUAL[0]), vmem(NZ * NW * 6),
            *[vmem(2 * c) for c in USUAL] * 2,
            vmem(NZ * NW * 6), vmem(NZ * NW * 6), vmem(5 * 64),
            pltpu.VMEM((384, 16, HD), jnp.bfloat16),
            pltpu.VMEM((384, 2048), jnp.bfloat16),
            pltpu.VMEM((BLK * 16, HD), jnp.float32),
            pltpu.VMEM((SEL * BLK, HD), jnp.bfloat16),
            pltpu.VMEM((SEL * BLK, 2 * HD), jnp.bfloat16),
            ints(NW, 1, 128), ints(4, 1, 128), ints(NW, 1, 128), ints(NW, 1, 128), ints(8, 128), ints(8, 128),
            pltpu.SMEM((8, 128), jnp.int32), pltpu.SMEM((8, 128), jnp.int32), pltpu.SMEM(asks.shape, jnp.int32),
            dma, dma((2, 2)), dma((2,)), dma((2, 2, 10)), dma((2, 2, 10)), dma((2, NZ)), dma((2,)), dma((2, NZ)),
            dma((NW + 4,)), dma((NW + 4,)), dma, dma, dma, dma, dma((16,)), dma((16,)), dma((3,)),
        ],
        compiler_params=pltpu.CompilerParams(
            collective_id=number, has_side_effects=True, vmem_limit_bytes=60 * 2**20
        ),
        name="fused",
    )(asks, within, block.astype(np.float32), lower, plane.astype(np.float32), counts, queries, k_own, v_own)


def full_plan(table):
    asked = table[:, :, :48].reshape(NZ, NW, NZ, 6)
    by_k = [jnp.roll(asked[:, :, k], -k, axis=0) for k in range(NZ)]
    up = [by_k[4][:, 0::2], by_k[3], by_k[2], by_k[1]]
    down = [by_k[4][:, 1::2], by_k[5], by_k[6], by_k[7]]
    lists = jnp.stack([jnp.concatenate([e.reshape(NZ, -1) for e in way], axis=1) for way in (up, down)])
    live = lists > 0
    size = lists.shape[2]
    before = jnp.asarray(np.triu(np.ones((size, size), np.float32), 1))
    at = jnp.dot(live.reshape(-1, size).astype(jnp.float32), before).astype(jnp.int32).reshape(lists.shape)
    hit = (at[:, 0, None, :] == jnp.arange(size)[None, :, None]) & live[:, 0, None, :]
    src = jnp.maximum(jnp.sum(jnp.where(hit, lists[:, 0, None, :], 0), axis=2) - 1, 0)

    def seg(d, k, part):
        lo, hi = (0, 24) if part == 0 else (24 + 48 * (part - 1), 24 + 48 * part)
        return jnp.minimum(at[d, (NZ - k) % NZ, lo:hi], FULL[3 - part] - 1) + d * FULL[3 - part]

    here = jnp.maximum(by_k[0][0] - 1, 0)
    four = jnp.stack([seg(0, 4, 0).reshape(4, 6), seg(1, 4, 0).reshape(4, 6)], axis=1)
    parts = [here, seg(0, 1, 3), seg(0, 2, 2), seg(0, 3, 1), four, seg(1, 5, 1), seg(1, 6, 2), seg(1, 7, 3)]
    return src, jnp.concatenate([p.reshape(NW, 6) for p in parts], axis=1)


def per_device(queries, keys, values, sel_blocks, sel_counts):
    k_own = keys.reshape(128, BLK, HD)
    v_own = values.reshape(128, BLK, HD)
    counts = sel_counts.reshape(-1)
    used = np.arange(SEL)[None, None, :] < sel_counts[:, :, None]
    asks = jnp.where(used, sel_blocks, -1).reshape(1, ITEMS * SEL)
    asks = jnp.pad(asks, ((0, 0), (0, 256 - ITEMS * SEL)), constant_values=-1)
    out, over, table, where = fused(1, asks, counts, queries, k_own, v_own)

    def again():
        src, post = full_plan(table)
        none = jnp.zeros((1, 128), jnp.int32)
        k, _ = exchange_tiles(2, FULL, src, post, none, (k_own,), (None,))
        v, _ = exchange_tiles(3, FULL, src, post, none, (v_own,), (None,))
        return attend_all(4, where[0, :ITEMS * SEL], counts, none, queries, k, v)[0]

    return lax.cond(over[0, 0] > 0, again, lambda: out)


def solution(mesh):
    placed = (
        P("ctx", "head", None),
        P("head", "ctx", None),
        P("head", "ctx", None),
        P("ctx", "head", None),
        P("ctx", "head"),
    )
    return jax.shard_map(
        per_device, mesh=mesh, in_specs=placed, out_specs=P(("ctx", "head"), None), check_vma=False
    )
```

```python
import jax
import jax.numpy as jnp
import numpy as np
from jax import lax
from jax.experimental import pallas as pl
from jax.experimental.pallas import tpu as pltpu
from jax.sharding import PartitionSpec as P

BLK = 64
HD = 128
SEL = 16
ITEMS = 12
NZ = 8
NW = 8
STEPS = 4
USUAL = (104, 78, 50, 24)
FULL = (168, 120, 72, 24)
MESH = pl.DeviceIdType.MESH


def at_ctx(index):
    return {"ctx": index}


def tiles_kernel(caps, arrays, fetch, src, post, over, *refs):
    cuts = (0, *caps[::-1])
    refs = list(refs)
    take = lambda n: [refs.pop(0) for _ in range(n)]
    owns = take(arrays)
    twins = [None if f else refs.pop(0) for f in fetch]
    outs, over_out = take(arrays), refs.pop(0)
    tab, lists, stage = take(arrays), take(arrays), take(arrays)
    hops = [take(STEPS) for _ in range(arrays)]
    overs, tab_sem, twin_send, z_send, z_recv, y_send, y_recv, y_local, over_send, over_recv = refs
    me = lax.axis_index("ctx")
    z, w = me // NW, me % NW
    core = me % 2
    twin_at = me + 1 - 2 * core
    towards = (((z + 1) % NZ) * NW + w, ((z + NZ - 1) % NZ) * NW + w)

    barrier = pltpu.get_barrier_semaphore()
    for other in towards:
        pl.semaphore_signal(barrier, inc=1, device_id=at_ctx(other), device_id_type=MESH)
    for r in range(1, NW):
        pl.semaphore_signal(barrier, inc=1, device_id=at_ctx(z * NW + (w + r) % NW), device_id_type=MESH)
    pl.semaphore_wait(barrier, NW + 1)

    loads = []
    for a in range(arrays):
        mine = tab[a].at[pl.ds(core * 128, 128)]
        pair = [pltpu.make_async_copy(owns[a], mine, tab_sem.at[a, 0])]
        if fetch[a]:
            pair.append(
                pltpu.make_async_remote_copy(
                    src_ref=owns[a], dst_ref=mine, send_sem=twin_send.at[a], recv_sem=tab_sem.at[a, 1],
                    device_id=at_ctx(twin_at), device_id_type=MESH,
                )
            )
        else:
            pair.append(
                pltpu.make_async_copy(twins[a], tab[a].at[pl.ds((1 - core) * 128, 128)], tab_sem.at[a, 1])
            )
        for copy in pair:
            copy.start()
        loads.append(pair)
    told = []
    for r in range(1, NW):
        copy = pltpu.make_async_remote_copy(
            src_ref=over, dst_ref=overs.at[r], send_sem=over_send.at[r], recv_sem=over_recv.at[r],
            device_id=at_ctx(z * NW + (w + r) % NW), device_id_type=MESH,
        )
        copy.start()
        told.append(copy)

    def hop(a, d, step, piece):
        lo, hi = cuts[piece], cuts[piece + 1]
        source = lists[a] if step == 1 else hops[a][step - 2]
        number = (0, 4, 7, 9)[step - 1] + piece
        return pltpu.make_async_remote_copy(
            src_ref=source.at[pl.ds(d * caps[max(step - 2, 0)] + lo, hi - lo)],
            dst_ref=hops[a][step - 1].at[pl.ds(d * caps[step - 1] + lo, hi - lo)],
            send_sem=z_send.at[a, d, number],
            recv_sem=z_recv.at[a, d, number],
            device_id=at_ctx(towards[d]),
            device_id_type=MESH,
        )

    def pack(a, piece):
        for d in range(2):
            def one(i, carry):
                lists[a][d * caps[0] + i] = tab[a][src[d, i]]
                return carry

            lax.fori_loop(cuts[piece], cuts[piece + 1], one, 0)

    def deliver(a, k):
        base = k * NW * 6
        source = tab[a] if k == 0 else hops[a][min(k, NZ - k) - 1]

        def one(i, carry):
            for j in range(6):
                stage[a][base + i * 6 + j] = source[post[i, k * 6 + j]]
            return carry

        lax.fori_loop(0, NW, one, 0)

        def send(r, carry):
            ow = (w + r) % NW
            pltpu.make_async_remote_copy(
                src_ref=stage[a].at[pl.ds(base + ow * 6, 6)],
                dst_ref=outs[a].at[pl.ds(base + w * 6, 6)],
                send_sem=y_send.at[a],
                recv_sem=y_recv.at[a],
                device_id=at_ctx(z * NW + ow),
                device_id_type=MESH,
            ).start()
            return carry

        lax.fori_loop(1, NW, send, 0)
        pltpu.make_async_copy(
            stage[a].at[pl.ds(base + w * 6, 6)], outs[a].at[pl.ds(base + w * 6, 6)], y_local.at[a]
        ).start()

    def arrive_and_pass(a, step):
        for piece in range(5 - step):
            for d in range(2):
                hop(a, d, step, piece).wait_recv()
                if piece < 4 - step:
                    hop(a, d, step + 1, piece).start()

    def start_first(a):
        for piece in range(STEPS):
            for d in range(2):
                hop(a, d, 1, piece).start()

    for copy in loads[0]:
        copy.wait()
    for piece in range(STEPS):
        pack(0, piece)
        for d in range(2):
            hop(0, d, 1, piece).start()
    if arrays == 2:
        for copy in loads[1]:
            copy.wait()
        for piece in range(STEPS):
            pack(1, piece)
    deliver(0, 0)
    arrive_and_pass(0, 1)
    if arrays == 2:
        start_first(1)
        deliver(1, 0)
    for a in range(arrays):
        if a:
            arrive_and_pass(a, 1)
        for step in range(1, STEPS):
            deliver(a, step)
            deliver(a, NZ - step)
            arrive_and_pass(a, step + 1)
        deliver(a, STEPS)
    for a in range(arrays):
        for d in range(2):
            for step in range(1, STEPS + 1):
                for piece in range(STEPS + 1 - step):
                    hop(a, d, step, piece).wait_send()
    most = over[...]
    for r, copy in enumerate(told):
        copy.wait()
        most = jnp.maximum(most, overs[r + 1])
    over_out[...] = most
    remote, local = NZ * (NW - 1) * 6, NZ * 6
    for a in range(arrays):
        pltpu.make_async_copy(stage[a].at[pl.ds(0, remote)], stage[a].at[pl.ds(0, remote)], y_send.at[a]).wait()
        pltpu.make_async_copy(outs[a].at[pl.ds(0, remote)], outs[a].at[pl.ds(0, remote)], y_recv.at[a]).wait()
        pltpu.make_async_copy(outs[a].at[pl.ds(0, local)], outs[a].at[pl.ds(0, local)], y_local.at[a]).wait()


def exchange_tiles(number, caps, src, post, over, owns, twins):
    n = len(owns)
    fetch = tuple(t is None for t in twins)
    given = [t for t in twins if t is not None]
    tiles = jax.ShapeDtypeStruct((NZ * NW * 6, BLK, HD), owns[0].dtype)
    vmem = lambda *shape: pltpu.VMEM((*shape, BLK, HD), jnp.bfloat16)
    smem, whole = pl.BlockSpec(memory_space=pltpu.SMEM), pl.BlockSpec(memory_space=pltpu.VMEM)
    anywhere = pl.BlockSpec(memory_space=pl.ANY)
    dma = pltpu.SemaphoreType.DMA
    return pl.pallas_call(
        lambda *refs: tiles_kernel(caps, n, fetch, *refs),
        out_shape=(*[tiles] * n, jax.ShapeDtypeStruct((1, 128), jnp.int32)),
        in_specs=[smem, smem, whole, *[anywhere] * (n + len(given))],
        out_specs=(*[anywhere] * n, whole),
        scratch_shapes=[
            *[vmem(256)] * n,
            *[vmem(2 * caps[0])] * n,
            *[vmem(NZ * NW * 6)] * n,
            *[vmem(2 * c) for c in caps] * n,
            pltpu.VMEM((NW, 1, 128), jnp.int32),
            dma((n, 2)), dma((n,)), dma((n, 2, 10)), dma((n, 2, 10)),
            dma((n,)), dma((n,)), dma((n,)), dma((NW,)), dma((NW,)),
        ],
        compiler_params=pltpu.CompilerParams(
            collective_id=number, has_side_effects=True, vmem_limit_bytes=60 * 2**20
        ),
        name="tiles",
    )(src, post, over, *owns, *given)


def attend_kernel(where, counts, over, q, k, v, out, over_out, merged, qf, kc, vc, overs, send_sem, recv_sem, own_sem, over_send, over_recv):
    me = lax.axis_index("head")
    barrier = pltpu.get_barrier_semaphore()
    for r in range(1, 4):
        pl.semaphore_signal(barrier, inc=1, device_id={"head": (me + r) % 4}, device_id_type=MESH)
    pl.semaphore_wait(barrier, 3)
    told = []
    for r in range(1, 4):
        copy = pltpu.make_async_remote_copy(
            src_ref=over, dst_ref=overs.at[r], send_sem=over_send.at[r], recv_sem=over_recv.at[r],
            device_id={"head": (me + r) % 4}, device_id_type=MESH,
        )
        copy.start()
        told.append(copy)
    keys = SEL * BLK
    factor = float(HD ** -0.5 * np.log2(np.e))
    vc[:, HD:] = jnp.ones((keys, HD), jnp.bfloat16)
    first = ((me + 1) * 3 // 2) % 6

    def one_block(i, carry):
        b = (first + i) % 6
        qf[...] = q[pl.ds(b * BLK, BLK)].astype(jnp.float32).reshape(BLK * 16, HD)
        for g in range(2):
            item = b * 2 + g

            def gather(s, c):
                at = where[item * SEL + s]
                kc[pl.ds(s * BLK, BLK)] = k[at]
                vc[pl.ds(s * BLK, BLK), 0:HD] = v[at]
                return c

            lax.fori_loop(0, SEL, gather, 0)
            rows = jnp.concatenate(
                [qf[pl.ds(g * 8 + h, BLK, stride=16)].astype(jnp.bfloat16) for h in range(8)], axis=0
            )
            s = lax.dot_general(rows, kc[...], (((1,), (1,)), ((), ())), preferred_element_type=jnp.float32)
            kept = lax.broadcasted_iota(jnp.int32, (1, keys), 1) < counts[item] * BLK
            s = jnp.where(kept, s, -jnp.inf)
            top = jnp.max(s, axis=1, keepdims=True)
            p = jnp.exp2((s - top) * factor).astype(jnp.bfloat16)
            o = jnp.dot(p, vc[...], preferred_element_type=jnp.float32)
            o = o[:, 0:HD] / o[:, HD:]
            for h in range(8):
                merged[pl.ds(b * BLK, BLK), pl.ds(g * 1024 + h * HD, HD)] = o[h * BLK:(h + 1) * BLK].astype(jnp.bfloat16)
        for half in range(2):
            unit = b * 2 + half
            to = unit // 3
            source = merged.at[pl.ds(unit * 32, 32)]
            target = out.at[pl.ds((unit % 3) * 32, 32), pl.ds(pl.multiple_of(me * 2048, 2048), 2048)]

            @pl.when(to == me)
            def _():
                pltpu.make_async_copy(source, target, own_sem).start()

            @pl.when(to != me)
            def _():
                pltpu.make_async_remote_copy(
                    src_ref=source, dst_ref=target, send_sem=send_sem, recv_sem=recv_sem,
                    device_id={"head": to}, device_id_type=MESH,
                ).start()
        return carry

    lax.fori_loop(0, 6, one_block, 0)
    most = over[...]
    for r, copy in enumerate(told):
        copy.wait()
        most = jnp.maximum(most, overs[r + 1])
    over_out[...] = most
    pltpu.make_async_copy(out.at[:, pl.ds(0, 2048)], out.at[:, pl.ds(0, 2048)], own_sem).wait()
    pltpu.make_async_copy(out.at[:, pl.ds(0, 6144)], out.at[:, pl.ds(0, 6144)], send_sem).wait()
    pltpu.make_async_copy(out.at[:, pl.ds(0, 6144)], out.at[:, pl.ds(0, 6144)], recv_sem).wait()


def attend_all(number, where, counts, over, queries, k, v):
    smem, vmem = pl.BlockSpec(memory_space=pltpu.SMEM), pl.BlockSpec(memory_space=pltpu.VMEM)
    dma = pltpu.SemaphoreType.DMA
    return pl.pallas_call(
        attend_kernel,
        out_shape=(jax.ShapeDtypeStruct((96, 8192), jnp.bfloat16), jax.ShapeDtypeStruct((1, 128), jnp.int32)),
        in_specs=[smem, smem, vmem, vmem, vmem, vmem],
        out_specs=(pl.BlockSpec(memory_space=pl.ANY), vmem),
        scratch_shapes=[
            pltpu.VMEM((384, 2048), jnp.bfloat16),
            pltpu.VMEM((BLK * 16, HD), jnp.float32),
            pltpu.VMEM((SEL * BLK, HD), jnp.bfloat16),
            pltpu.VMEM((SEL * BLK, 2 * HD), jnp.bfloat16),
            pltpu.VMEM((4, 1, 128), jnp.int32),
            dma, dma, dma, dma((4,)), dma((4,)),
        ],
        compiler_params=pltpu.CompilerParams(
            collective_id=number, has_side_effects=True, vmem_limit_bytes=60 * 2**20
        ),
        name="attend",
    )(where, counts, over, queries, k, v)


def fused_kernel(
    asks, within, same, lower, column, counts, q_in, k_own, v_own, out, over_out, table, where_v,
    tab_k, tab_v, packed, stage, k1, k2, k3, k4, v1, v2, v3, v4, land_k, land_v, more,
    q, merged, qf, kc, vc, overs, overs_head, mine, rows, src_v, post_v, src, post, where,
    q_sem, tab_sem, twin_send, z_send, z_recv, y_send, y_recv, y_local,
    over_send, over_recv, out_send, out_recv, out_own, local_sem, ask_send, ask_recv, plan_sem,
):
    caps = USUAL
    cuts = (0, *caps[::-1])
    tab, land, hops = (tab_k, tab_v), (land_k, land_v), ((k1, k2, k3, k4), (v1, v2, v3, v4))
    me = lax.axis_index("ctx")
    head = lax.axis_index("head")
    z, w = me // NW, me % NW
    core = me % 2
    towards = (((z + 1) % NZ) * NW + w, ((z + NZ - 1) % NZ) * NW + w)

    barrier = pltpu.get_barrier_semaphore()
    for r in range(1, 8):
        pl.semaphore_signal(barrier, inc=1, device_id=at_ctx(z * NW + (w + r) % NW), device_id_type=MESH)
        pl.semaphore_signal(barrier, inc=1, device_id=at_ctx((z + r) % NZ * NW + w), device_id_type=MESH)
    for r in range(1, 4):
        pl.semaphore_signal(barrier, inc=1, device_id={"head": (head + r) % 4}, device_id_type=MESH)

    size = asks.shape[1]
    ask = asks[...]
    across = jnp.broadcast_to(ask.astype(jnp.float32), (size, size))
    down = across.T.astype(jnp.int32)
    i0 = lax.broadcasted_iota(jnp.int32, (size, size), 0)
    i1 = lax.broadcasted_iota(jnp.int32, (size, size), 1)
    earlier = ((down >> 6) == (jnp.broadcast_to(ask, (size, size)) >> 6)) & (i0 < i1)
    rank = jnp.sum(earlier.astype(jnp.float32), axis=0, keepdims=True).astype(jnp.int32)
    used = ask >= 0
    holder = ask >> 6
    its_core = holder & 1
    lane = ((holder >> 1) & 3) * 2 + ((rank + its_core) & 1)
    away = (z - (holder >> 3) + NZ) & 7
    inside = its_core * 3 + (rank >> 1)
    group = (lax.broadcasted_iota(jnp.int32, (1, size), 1) >> 4) & 1
    tile = its_core * 128 + group * BLK + (ask & 63) + 1
    where_v[...] = jnp.clip(jnp.where(used, away * 48 + lane * 6 + inside, 0), 0, NZ * NW * 6 - 1)
    to_lane = lax.broadcasted_iota(jnp.int32, (NW, size), 0) == jnp.where(used, lane, -1)
    to_slot = lax.broadcasted_iota(jnp.int32, (128, size), 0) == away * 6 + inside
    asked_of = lax.dot_general(
        jnp.where(to_lane, tile.astype(jnp.float32), 0.0), to_slot.astype(jnp.float32),
        (((1,), (1,)), ((), ())), preferred_element_type=jnp.float32,
    ).astype(jnp.int32)
    for i in range(NW):
        mine[i] = asked_of[i:i + 1]

    pl.semaphore_wait(barrier, 17)

    asking = []
    for r in range(1, NW):
        ow = (w + r) % NW
        copy = pltpu.make_async_remote_copy(
            src_ref=mine.at[pl.ds(ow, 1)], dst_ref=rows.at[pl.ds(w, 1)],
            send_sem=ask_send.at[r], recv_sem=ask_recv.at[r],
            device_id=at_ctx(z * NW + ow), device_id_type=MESH,
        )
        copy.start()
        asking.append(copy)
    own = pltpu.make_async_copy(mine.at[pl.ds(w, 1)], rows.at[pl.ds(w, 1)], local_sem)
    own.start()

    mine_k, mine_v = (t.at[pl.ds(core * 128, 128)] for t in tab)
    loads = []
    for a, (ref, near) in enumerate(((k_own, mine_k), (v_own, mine_v))):
        pair = (
            pltpu.make_async_copy(ref, near, tab_sem.at[a, 0]),
            pltpu.make_async_remote_copy(
                src_ref=ref, dst_ref=near, send_sem=twin_send.at[a], recv_sem=tab_sem.at[a, 1],
                device_id=at_ctx(me + 1 - 2 * core), device_id_type=MESH,
            ),
        )
        for copy in pair:
            copy.start()
        loads.append(pair)
    q_load = pltpu.make_async_copy(q_in, q, q_sem)
    q_load.start()

    own.wait()
    for copy in asking:
        copy.wait()
    table[0] = jnp.concatenate([rows[i] for i in range(NW)], axis=0)
    asking = []
    for r in range(1, NZ):
        copy = pltpu.make_async_remote_copy(
            src_ref=table.at[0], dst_ref=table.at[NZ - r],
            send_sem=ask_send.at[NW + r], recv_sem=ask_recv.at[NW + r],
            device_id=at_ctx((z + r) % NZ * NW + w), device_id_type=MESH,
        )
        copy.start()
        asking.append(copy)
    for copy in asking:
        copy.wait()

    kind = (lax.broadcasted_iota(jnp.int32, (NW, 128), 1) * 43) >> 8
    asked = [table[i] for i in range(NZ)]
    by_source = []
    for i in range(NZ):
        row = jnp.zeros((NW, 128), jnp.int32)
        for k in range(NZ):
            row = jnp.where(kind == k, asked[(i + k) % NZ], row)
        by_source.append(row)
    tiles = jnp.concatenate(by_source, axis=0)
    kind = jnp.concatenate([kind] * NZ, axis=0)
    live = tiles > 0
    ones = live.astype(jnp.float32)
    dot = lambda x, y: jnp.dot(x, y, preferred_element_type=jnp.float32)
    per_row = dot(ones, same[...])
    at = dot(ones, within[...]) + dot(lower[...], per_row)
    sums = dot(column[...], per_row)
    n = [sums[:, 6 * k:6 * k + 1] for k in range(NZ)]
    c1, c2, c3, c4 = (float(c) for c in USUAL)
    least = lambda x, y, t: jnp.minimum(
        jnp.minimum(jnp.full_like(x, c4), c3 - x), jnp.minimum(c2 - x - y, c1 - x - y - t)
    )
    room_up, room_down = least(n[3], n[2], n[1]), least(n[5], n[6], n[7])
    four_up = jnp.clip(room_up, 0.0, n[4])
    four_down = n[4] - four_up
    short = (room_up < 0) | (room_down < 0) | (four_down > room_down)
    over = jnp.broadcast_to(jnp.max(short.astype(jnp.float32), axis=0, keepdims=True), (1, 128)).astype(jnp.int32)
    up = (kind < 4) | ((kind == 4) & (at < four_up))
    base = jnp.zeros_like(at)
    for k, first in (
        (3, four_up), (2, four_up + n[3]), (1, four_up + n[3] + n[2]),
        (5, four_down), (6, four_down + n[5]), (7, four_down + n[5] + n[6]),
    ):
        base = jnp.where(kind == k, first, base)
    base = jnp.where((kind == 4) & (at >= four_up), -four_up, base)
    at = at + base

    places = lax.broadcasted_iota(jnp.int32, (128, 128), 0).astype(jnp.float32)
    found = []
    for way in range(2):
        mine_too = live[0:NW] & (up[0:NW] if way == 0 else ~up[0:NW]) & (kind[0:NW] > 0)
        place = jnp.where(mine_too, at[0:NW], -1.0)
        value = jnp.where(mine_too, tiles[0:NW], 0).astype(jnp.float32)
        total = jnp.zeros((128, 128), jnp.float32)
        for i in range(NW):
            total = jnp.where(place[i:i + 1] == places, value[i:i + 1], total)
        found.append(
            lax.dot_general(
                jnp.ones((8, 128), jnp.float32), total, (((1,), (1,)), ((), ())), preferred_element_type=jnp.float32
            )
        )
    row = lax.broadcasted_iota(jnp.int32, (8, 128), 0)
    src_v[...] = jnp.clip(jnp.where(row == 0, found[0], found[1]).astype(jnp.int32) - 1, 0, 255)

    cap = jnp.full((NZ * NW, 128), USUAL[0], jnp.int32)
    for k in range(2, 7):
        cap = jnp.where(kind == k, USUAL[min(k, NZ - k) - 1], cap)
    spot = jnp.clip(at.astype(jnp.int32), 0, cap - 1) + jnp.where(up, 0, cap)
    mine_at = jnp.clip(tiles[0:NW] - 1, 0, 255)
    for k in range(1, NZ):
        i = NZ - k
        mine_at = jnp.where(kind[0:NW] == k, spot[i * NW:(i + 1) * NW], mine_at)
    post_v[...] = mine_at
    moves = [
        pltpu.make_async_copy(ref, to, plan_sem.at[i])
        for i, (ref, to) in enumerate(((src_v, src), (post_v, post), (where_v, where)))
    ]
    for copy in moves:
        copy.start()
    for copy in moves:
        copy.wait()
    overs[0] = over
    told = []
    for r in range(1, NW):
        copy = pltpu.make_async_remote_copy(
            src_ref=overs.at[0], dst_ref=overs.at[r], send_sem=over_send.at[r], recv_sem=over_recv.at[r],
            device_id=at_ctx(z * NW + (w + r) % NW), device_id_type=MESH,
        )
        copy.start()
        told.append(copy)

    def hop(a, d, step, piece):
        lo, hi = cuts[piece], cuts[piece + 1]
        source = packed if step == 1 else hops[a][step - 2]
        number = (0, 4, 7, 9)[step - 1] + piece
        return pltpu.make_async_remote_copy(
            src_ref=source.at[pl.ds(d * caps[max(step - 2, 0)] + lo, hi - lo)],
            dst_ref=hops[a][step - 1].at[pl.ds(d * caps[step - 1] + lo, hi - lo)],
            send_sem=z_send.at[a, d, number],
            recv_sem=z_recv.at[a, d, number],
            device_id=at_ctx(towards[d]),
            device_id_type=MESH,
        )

    def pack_and_start(a):
        for piece in range(STEPS):
            for d in range(2):
                def one(i, carry):
                    packed[d * caps[0] + i] = tab[a][src[d, i]]
                    return carry

                lax.fori_loop(cuts[piece], cuts[piece + 1], one, 0)
                hop(a, d, 1, piece).start()

    def settle(a, k):
        pltpu.make_async_copy(stage.at[pl.ds(0, 42)], stage.at[pl.ds(0, 42)], y_send.at[a, k]).wait()
        pltpu.make_async_copy(stage.at[pl.ds(0, 6)], stage.at[pl.ds(0, 6)], y_local.at[a, k]).wait()

    def deliver(a, k):
        base = k * NW * 6
        source = tab[a] if k == 0 else hops[a][min(k, NZ - k) - 1]
        if a and k != STEPS:
            settle(0, k)

        def one(i, carry):
            for j in range(6):
                stage[base + i * 6 + j] = source[post[i, k * 6 + j]]
            return carry

        lax.fori_loop(0, NW, one, 0)

        def send(r, carry):
            ow = (w + r) % NW
            pltpu.make_async_remote_copy(
                src_ref=stage.at[pl.ds(base + ow * 6, 6)],
                dst_ref=land[a].at[pl.ds(base + w * 6, 6)],
                send_sem=y_send.at[a, k],
                recv_sem=y_recv.at[a],
                device_id=at_ctx(z * NW + ow),
                device_id_type=MESH,
            ).start()
            return carry

        lax.fori_loop(1, NW, send, 0)
        pltpu.make_async_copy(
            stage.at[pl.ds(base + w * 6, 6)], land[a].at[pl.ds(base + w * 6, 6)], y_local.at[a, k]
        ).start()

    def arrive_and_pass(a, step):
        for piece in range(5 - step):
            for d in range(2):
                hop(a, d, step, piece).wait_recv()
                if piece < 4 - step:
                    hop(a, d, step + 1, piece).start()

    def all_landed(a):
        remote = NZ * (NW - 1) * 6
        pltpu.make_async_copy(land[a].at[pl.ds(0, remote)], land[a].at[pl.ds(0, remote)], y_recv.at[a]).wait()

    keys = SEL * BLK
    factor = float(HD ** -0.5 * np.log2(np.e))
    first = ((head + 1) * 3 // 2) % 6 * 2

    def item_of(n):
        i = n // 2
        return (first + (i * 3 + i // 2) % 6 * 2 + n % 2) % ITEMS

    def weigh(ref, n, spot):
        item = item_of(n)
        b, g = item // 2, item % 2
        qf[...] = q[pl.ds(b * BLK, BLK)].astype(jnp.float32).reshape(BLK * 16, HD)

        def gather(i, c):
            kc[pl.ds(i * BLK, BLK)] = land_k[where[0, item * SEL + i]]
            return c

        lax.fori_loop(0, SEL, gather, 0)
        rows = jnp.concatenate(
            [qf[pl.ds(g * 8 + h, BLK, stride=16)].astype(jnp.bfloat16) for h in range(8)], axis=0
        )
        s = lax.dot_general(rows, kc[...], (((1,), (1,)), ((), ())), preferred_element_type=jnp.float32)
        kept = lax.broadcasted_iota(jnp.int32, (1, keys), 1) < counts[item] * BLK
        s = jnp.where(kept, s, -jnp.inf)
        top = jnp.max(s, axis=1, keepdims=True)
        p = jnp.exp2((s - top) * factor).astype(jnp.bfloat16)
        for h in range(8):
            for c in range(8):
                ref[spot * 64 + h * 8 + c] = p[h * BLK:(h + 1) * BLK, c * HD:(c + 1) * HD]

    def finish(ref, n, spot):
        item = item_of(n)
        b, g = item // 2, item % 2

        def gather(i, c):
            vc[pl.ds(i * BLK, BLK), 0:HD] = land_v[where[0, item * SEL + i]]
            return c

        lax.fori_loop(0, SEL, gather, 0)
        p = jnp.concatenate(
            [jnp.concatenate([ref[spot * 64 + h * 8 + c] for c in range(8)], axis=1) for h in range(8)], axis=0
        )
        o = jnp.dot(p, vc[...], preferred_element_type=jnp.float32)
        o = (o[:, 0:HD] / o[:, HD:]).astype(jnp.bfloat16)
        for h in range(8):
            merged[pl.ds(b * BLK, BLK), pl.ds(pl.multiple_of(g * 1024 + h * HD, HD), HD)] = o[h * BLK:(h + 1) * BLK]

        @pl.when(g == 1)
        def _():
            for half in range(2):
                unit = b * 2 + half
                to = unit // 3
                source = merged.at[pl.ds(unit * 32, 32)]
                target = out.at[pl.ds((unit % 3) * 32, 32), pl.ds(pl.multiple_of(head * 2048, 2048), 2048)]

                @pl.when(to == head)
                def _():
                    pltpu.make_async_copy(source, target, out_own).start()

                @pl.when(to != head)
                def _():
                    pltpu.make_async_remote_copy(
                        src_ref=source, dst_ref=target, send_sem=out_send, recv_sem=out_recv,
                        device_id={"head": to}, device_id_type=MESH,
                    ).start()

    def over_items(work, ref, lo, hi):
        def one(n, carry):
            work(ref, n, n - lo)
            return carry

        lax.fori_loop(lo, hi, one, 0)

    for copy in loads[0]:
        copy.wait()
    pack_and_start(0)
    deliver(0, 0)
    arrive_and_pass(0, 1)
    for piece in range(STEPS):
        for d in range(2):
            hop(0, d, 1, piece).wait_send()
    for copy in loads[1]:
        copy.wait()
    pack_and_start(1)
    deliver(1, 0)
    deliver(0, 1)
    deliver(0, 7)
    arrive_and_pass(0, 2)
    deliver(0, 2)
    deliver(0, 6)
    arrive_and_pass(1, 1)
    deliver(1, 1)
    deliver(1, 7)
    arrive_and_pass(0, 3)
    deliver(0, 3)
    deliver(0, 5)
    arrive_and_pass(1, 2)
    deliver(1, 2)
    deliver(1, 6)
    arrive_and_pass(0, 4)
    deliver(0, 4)
    for step in range(2, STEPS + 1):
        for piece in range(STEPS + 1 - step):
            for d in range(2):
                hop(0, d, step, piece).wait_send()
    arrive_and_pass(1, 3)
    deliver(1, 3)
    deliver(1, 5)
    vc[:, HD:] = jnp.ones((keys, HD), jnp.bfloat16)
    q_load.wait()
    most = over
    for r, copy in enumerate(told):
        copy.wait()
        most = jnp.maximum(most, overs[r + 1])
    overs_head[0] = most
    told = []
    for r in range(1, 4):
        copy = pltpu.make_async_remote_copy(
            src_ref=overs_head.at[0], dst_ref=overs_head.at[r], send_sem=over_send.at[NW + r], recv_sem=over_recv.at[NW + r],
            device_id={"head": (head + r) % 4}, device_id_type=MESH,
        )
        copy.start()
        told.append(copy)
    settle(0, STEPS)
    all_landed(0)
    over_items(weigh, tab_k, 0, 4)
    arrive_and_pass(1, 4)
    deliver(1, 4)
    over_items(weigh, k1, 4, 7)
    over_items(weigh, more, 7, ITEMS)
    for step in range(1, STEPS + 1):
        for piece in range(STEPS + 1 - step):
            for d in range(2):
                hop(1, d, step, piece).wait_send()
    for k in range(NZ):
        settle(1, k)
    all_landed(1)
    over_items(finish, tab_k, 0, 4)
    over_items(finish, k1, 4, 7)
    over_items(finish, more, 7, ITEMS)
    for r, copy in enumerate(told):
        copy.wait()
        most = jnp.maximum(most, overs_head[r + 1])
    over_out[...] = most
    pltpu.make_async_copy(out.at[:, pl.ds(0, 2048)], out.at[:, pl.ds(0, 2048)], out_own).wait()
    pltpu.make_async_copy(out.at[:, pl.ds(0, 6144)], out.at[:, pl.ds(0, 6144)], out_send).wait()
    pltpu.make_async_copy(out.at[:, pl.ds(0, 6144)], out.at[:, pl.ds(0, 6144)], out_recv).wait()


def fused(number, asks, counts, queries, k_own, v_own):
    vmem = lambda *shape: pltpu.VMEM((*shape, BLK, HD), jnp.bfloat16)
    ints = lambda *shape: pltpu.VMEM(shape, jnp.int32)
    smem, whole = pl.BlockSpec(memory_space=pltpu.SMEM), pl.BlockSpec(memory_space=pltpu.VMEM)
    anywhere = pl.BlockSpec(memory_space=pl.ANY)
    dma = pltpu.SemaphoreType.DMA
    lane, row = np.arange(128), np.arange(NZ * NW)
    block = (lane[:, None] // 6 == lane[None, :] // 6) & (lane[:, None] < 48)
    plane = row[:, None] // NW == row[None, :] // NW
    within = (block & (lane[:, None] < lane[None, :])).astype(np.float32)
    lower = (plane & (row[None, :] < row[:, None])).astype(np.float32)
    return pl.pallas_call(
        fused_kernel,
        out_shape=(
            jax.ShapeDtypeStruct((96, 8192), jnp.bfloat16),
            jax.ShapeDtypeStruct((1, 128), jnp.int32),
            jax.ShapeDtypeStruct((NZ, NW, 128), jnp.int32),
            jax.ShapeDtypeStruct(asks.shape, jnp.int32),
        ),
        in_specs=[*[whole] * 5, smem, *[anywhere] * 3],
        out_specs=(anywhere, whole, whole, whole),
        scratch_shapes=[
            vmem(256), vmem(256), vmem(2 * USUAL[0]), vmem(NZ * NW * 6),
            *[vmem(2 * c) for c in USUAL] * 2,
            vmem(NZ * NW * 6), vmem(NZ * NW * 6), vmem(5 * 64),
            pltpu.VMEM((384, 16, HD), jnp.bfloat16),
            pltpu.VMEM((384, 2048), jnp.bfloat16),
            pltpu.VMEM((BLK * 16, HD), jnp.float32),
            pltpu.VMEM((SEL * BLK, HD), jnp.bfloat16),
            pltpu.VMEM((SEL * BLK, 2 * HD), jnp.bfloat16),
            ints(NW, 1, 128), ints(4, 1, 128), ints(NW, 1, 128), ints(NW, 1, 128), ints(8, 128), ints(8, 128),
            pltpu.SMEM((8, 128), jnp.int32), pltpu.SMEM((8, 128), jnp.int32), pltpu.SMEM(asks.shape, jnp.int32),
            dma, dma((2, 2)), dma((2,)), dma((2, 2, 10)), dma((2, 2, 10)), dma((2, NZ)), dma((2,)), dma((2, NZ)),
            dma((NW + 4,)), dma((NW + 4,)), dma, dma, dma, dma, dma((16,)), dma((16,)), dma((3,)),
        ],
        compiler_params=pltpu.CompilerParams(
            collective_id=number, has_side_effects=True, vmem_limit_bytes=60 * 2**20
        ),
        name="fused",
    )(asks, within, block.astype(np.float32), lower, plane.astype(np.float32), counts, queries, k_own, v_own)


def full_plan(table):
    asked = table[:, :, :48].reshape(NZ, NW, NZ, 6)
    by_k = [jnp.roll(asked[:, :, k], -k, axis=0) for k in range(NZ)]
    up = [by_k[4][:, 0::2], by_k[3], by_k[2], by_k[1]]
    down = [by_k[4][:, 1::2], by_k[5], by_k[6], by_k[7]]
    lists = jnp.stack([jnp.concatenate([e.reshape(NZ, -1) for e in way], axis=1) for way in (up, down)])
    live = lists > 0
    size = lists.shape[2]
    before = jnp.asarray(np.triu(np.ones((size, size), np.float32), 1))
    at = jnp.dot(live.reshape(-1, size).astype(jnp.float32), before).astype(jnp.int32).reshape(lists.shape)
    hit = (at[:, 0, None, :] == jnp.arange(size)[None, :, None]) & live[:, 0, None, :]
    src = jnp.maximum(jnp.sum(jnp.where(hit, lists[:, 0, None, :], 0), axis=2) - 1, 0)

    def seg(d, k, part):
        lo, hi = (0, 24) if part == 0 else (24 + 48 * (part - 1), 24 + 48 * part)
        return jnp.minimum(at[d, (NZ - k) % NZ, lo:hi], FULL[3 - part] - 1) + d * FULL[3 - part]

    here = jnp.maximum(by_k[0][0] - 1, 0)
    four = jnp.stack([seg(0, 4, 0).reshape(4, 6), seg(1, 4, 0).reshape(4, 6)], axis=1)
    parts = [here, seg(0, 1, 3), seg(0, 2, 2), seg(0, 3, 1), four, seg(1, 5, 1), seg(1, 6, 2), seg(1, 7, 3)]
    return src, jnp.concatenate([p.reshape(NW, 6) for p in parts], axis=1)


def per_device(queries, keys, values, sel_blocks, sel_counts):
    k_own = keys.reshape(128, BLK, HD)
    v_own = values.reshape(128, BLK, HD)
    counts = sel_counts.reshape(-1)
    used = np.arange(SEL)[None, None, :] < sel_counts[:, :, None]
    asks = jnp.where(used, sel_blocks, -1).reshape(1, ITEMS * SEL)
    asks = jnp.pad(asks, ((0, 0), (0, 256 - ITEMS * SEL)), constant_values=-1)
    out, over, table, where = fused(1, asks, counts, queries, k_own, v_own)

    def again():
        src, post = full_plan(table)
        none = jnp.zeros((1, 128), jnp.int32)
        k, _ = exchange_tiles(2, FULL, src, post, none, (k_own,), (None,))
        v, _ = exchange_tiles(3, FULL, src, post, none, (v_own,), (None,))
        return attend_all(4, where[0, :ITEMS * SEL], counts, none, queries, k, v)[0]

    return lax.cond(over[0, 0] > 0, again, lambda: out)


def solution(mesh):
    placed = (
        P("ctx", "head", None),
        P("head", "ctx", None),
        P("head", "ctx", None),
        P("ctx", "head", None),
        P("ctx", "head"),
    )
    return jax.shard_map(
        per_device, mesh=mesh, in_specs=placed, out_specs=P(("ctx", "head"), None), check_vma=False
    )
```
